32 devices in a mesh: grp: 2 (over x), inp: 4 (over y, core), out: 4 (over z).
Axes of the slice: x: 2, y: 2, z: 4, core: 2. Of those that a mesh axis runs over, the one named last changes fastest.
Arguments:
- activations: bfloat16 [4, 512, 8192], P('grp', 'out', 'inp'), parts along dimension 0, may hold values from -6 to 6
- out_grads: bfloat16 [4, 512, 28672], P('grp', 'inp', 'out'), parts along dimension 0, may hold values from -6 to 6
- query_grads: bfloat16 [2, 28672, 8192], P(None, 'out', 'inp'), may hold values from -0.00036621094 to 0.00036621094
- token_ids: int32 [4, 512], P('grp'), parts along dimension 0, may hold values from 0 to 128255
- loss_mask: int32 [4, 512], P('grp'), parts along dimension 0, may hold values 0 or 1
Outputs:
- scores: float32 [2, 4, 512], P(None, 'grp'), parts along dimension 1
The draws below stay inside these ranges and needn't reach their ends.
There are 2 independent parts, one for each index of `grp`. The reference program is written for one: setup_inputs(seed, part) draws one part's arguments, and reference() takes and returns one part's arrays. A program takes and returns all parts, laid end to end along the dimension named above; an argument that names none is the same for every part. Nothing has to cross between parts.
All inputs are finite; a program needn't handle non-finite values.
Results may differ from the reference program's by a relative error of at most 0.0003.
Values may be sent and summed in bfloat16 or wider, within the bound.
No kernel may reach another device: no remote copies, remote signals or barrier semaphores. Data moves between devices by JAX's collectives and lax.ppermute only.
A program may use at most 128 MiB of HBM per device.

```python
import math
import jax
import jax.numpy as jnp
import numpy as np

D = 8192
FF = 28672
VOCAB = 128256
NQ = 2
BLOCK_TOK = 512
BLOCKS = 2


def set_ends(drawn, rng, smallest, top_value):
    spot = [jax.random.randint(jax.random.fold_in(rng, axis), (), 0, length) for axis, length in enumerate(drawn.shape)]
    main_axis = drawn.shape.index(max(drawn.shape))
    beside = spot[:main_axis] + [(spot[main_axis] + 1) % drawn.shape[main_axis]] + spot[main_axis + 1:]
    return drawn.at[tuple(spot)].set(smallest).at[tuple(beside)].set(top_value)


def level_of(key, shape, shards, low, top_value):
    loudness = 1.0
    for axis_at, parts in shards:
        steps = jax.random.uniform(jax.random.fold_in(jax.random.fold_in(key, 6), axis_at), (parts,), jnp.float32, low / len(shards), top_value / len(shards))
        loudness = loudness * jnp.repeat(jnp.exp(steps), shape[axis_at] // parts).reshape((-1,) + (1,) * (len(shape) - 1 - axis_at))
    return loudness


def wide_ids(stream_key, shape, number_of, lean):
    portions = [min(1 << octave, number_of + 1 - (1 << octave)) * (1 << 20) // math.isqrt((1 << octave) ** lean) + 1 for octave in range((number_of + 1).bit_length()) if 1 << octave <= number_of]
    scale = 1 + sum(portions) // (1 << 30)
    grid = np.cumsum(np.array([max(1, weight // scale) for weight in portions]))
    lot = jax.random.randint(jax.random.fold_in(stream_key, 1), shape, 0, int(grid[len(portions) - 1]))
    start = jnp.left_shift(1, jnp.searchsorted(jnp.asarray(grid, jnp.int32), lot, side="right").astype(jnp.int32))
    grade = start - 1 + jax.random.randint(jax.random.fold_in(stream_key, 4), shape, 0, 1 << 30) % jnp.minimum(start, number_of + 1 - start)
    return jax.random.permutation(jax.random.fold_in(stream_key, 2), number_of)[grade].astype(jnp.int32)


def scatter_about(own_key, shape, width, most, cuts=(), kind=jnp.bfloat16):
    result = width * jax.random.normal(own_key, shape, jnp.float32)
    if cuts:
        result = result * level_of(own_key, shape, cuts, -0.22, 0.18)
    return jnp.clip(result, -most, most).astype(kind)


def setup_inputs(seed: int = 0, part: int = 0) -> dict:
    splits = jax.random.split(jax.random.key(seed), 6)
    own_keys = jax.random.split(jax.random.fold_in(splits[5], part), 6)
    activations = scatter_about(own_keys[0], (BLOCKS, BLOCK_TOK, D), 1.0, 6.0, ((1, 4), (2, 4)))
    out_grads = scatter_about(own_keys[1], (BLOCKS, BLOCK_TOK, FF), 1.0, 6.0, ((1, 4), (2, 4)))
    query_grads = scatter_about(splits[2], (NQ, FF, D), (FF * D) ** -0.5, 0.00036621094, ((1, 4), (2, 4)))
    token_ids = set_ends(wide_ids(own_keys[3], (BLOCKS, BLOCK_TOK), VOCAB, 2), jax.random.fold_in(own_keys[3], 3), 0, VOCAB - 1).astype(jnp.int32)
    loss_mask = set_ends((jax.random.randint(own_keys[4], (BLOCKS, BLOCK_TOK), 0, 4) < 3).astype(jnp.int32), jax.random.fold_in(own_keys[4], 1), 0, 1)
    return {"activations": activations, "out_grads": out_grads, "query_grads": query_grads, "token_ids": token_ids, "loss_mask": loss_mask}


def reference(activations, out_grads, query_grads, token_ids, loss_mask):
    equal = token_ids[:, :, None] == token_ids[:, None, :]
    counts = jnp.sum(equal.astype(jnp.int32), axis=2)
    weight = loss_mask.astype(jnp.float32) / counts.astype(jnp.float32)
    per_block = []
    for number in range(BLOCKS):
        per_query = []
        for query in range(NQ):
            projected = jnp.dot(out_grads[number], query_grads[query], preferred_element_type=jnp.float32)
            per_query.append(jnp.sum(projected * activations[number].astype(jnp.float32), axis=1))
        per_block.append(jnp.stack(per_query, axis=1))
    raw = jnp.stack(per_block)
    return jnp.transpose(raw * weight[:, :, None], (2, 0, 1))
```

```python
import functools

import jax
import jax.numpy as jnp
from jax import lax
from jax.experimental import pallas as pl
from jax.experimental.pallas import tpu as pltpu
from jax.sharding import PartitionSpec as P

VMEM_LIMIT = 40 * 1024 * 1024


def matmul_kernel(parts, accumulate, *refs):
    g_refs, refs = refs[:parts], refs[parts:]
    q_ref, refs = refs[0], refs[1:]
    if accumulate:
        before_ref, refs = refs[0], refs[1:]
    out_ref, x_ref, sems = refs
    rows = x_ref.shape[0] // parts

    @pl.when((pl.program_id(0) == 0) & (pl.program_id(1) == 0))
    def _():
        copies = [
            pltpu.make_async_copy(g_ref, x_ref.at[pl.ds(at * rows, rows)], sems.at[at])
            for at, g_ref in enumerate(g_refs)
        ]
        for copy in copies:
            copy.start()
        for copy in copies:
            copy.wait()

    product = jnp.dot(x_ref[...], q_ref[0], preferred_element_type=jnp.float32)
    if accumulate:
        product = product + before_ref[0]
    out_ref[0] = product


def tile_of(length, most):
    size = min(length, most)
    while length % size:
        size -= 128
    return size


def project(parts, query_grads, chunk, before=None, tile=512):
    rows, depth = parts[0].shape
    queries, _, width = query_grads.shape
    tile = tile_of(width, tile)
    total = rows * len(parts)
    out_spec = pl.BlockSpec((1, total, tile), lambda q, i: (q, 0, i))
    in_specs = [pl.BlockSpec(memory_space=pl.ANY)] * len(parts)
    in_specs.append(pl.BlockSpec((1, depth, tile), lambda q, i: (q, chunk, i)))
    operands = [*parts, query_grads]
    aliases = {}
    if before is not None:
        aliases = {len(operands): 0}
        in_specs.append(out_spec)
        operands.append(before)
    return pl.pallas_call(
        functools.partial(matmul_kernel, len(parts), before is not None),
        grid=(queries, width // tile),
        in_specs=in_specs,
        out_specs=out_spec,
        out_shape=jax.ShapeDtypeStruct((queries, total, width), jnp.float32),
        scratch_shapes=[
            pltpu.VMEM((total, depth), jnp.bfloat16),
            pltpu.SemaphoreType.DMA((len(parts),)),
        ],
        input_output_aliases=aliases,
        cost_estimate=pl.CostEstimate(
            flops=2 * queries * total * depth * width,
            bytes_accessed=2 * queries * depth * width + 4 * queries * total * width * (1 + len(aliases)),
            transcendentals=0,
        ),
        compiler_params=pltpu.CompilerParams(vmem_limit_bytes=VMEM_LIMIT),
        name="project",
    )(*operands)


def xor_sum(value, axis, size):
    if size & (size - 1):
        return lax.psum(value, axis)
    terms = [value]
    for other in range(1, size):
        terms.append(lax.ppermute(value, axis, [(at, at ^ other) for at in range(size)]))
    while len(terms) > 1:
        terms = [terms[at] + terms[at + 1] for at in range(0, len(terms), 2)]
    return terms[0]


def shards(inp_size, out_size, activations, out_grads, query_grads, token_ids, loss_mask):
    blocks, shard, depth = out_grads.shape
    queries, _, width = query_grads.shape
    tokens = token_ids.shape[1]
    pair = 2 if inp_size % 2 == 0 else 1
    chips = inp_size // pair
    me = lax.axis_index("inp")
    chunks = 4 if depth % 512 == 0 else 1
    part = depth // chunks

    def flip(value):
        return lax.ppermute(value, "inp", [(at, at ^ 1) for at in range(inp_size)])

    def shift(value, by):
        return lax.ppermute(value, "inp", [(at, (at + pair * by) % inp_size) for at in range(inp_size)])

    own = out_grads.reshape(blocks * shard, depth)
    arrived = []
    for chunk in range(chunks):
        piece = own[:, chunk * part:(chunk + 1) * part]
        if chunk >= 2:
            piece, _ = lax.optimization_barrier((piece, arrived[chunk - 2]))
        arrived.append([shift(piece, by) for by in range(1, chips)])
    near = [own] + ([flip(own)] if pair == 2 else [])
    gathered = lax.all_gather(activations, "out", axis=1, tiled=True)

    near_sum = project(near, query_grads, 0, tile=256)
    far_sum = None
    if chips > 1:
        for chunk in range(chunks):
            far = []
            for piece in arrived[chunk]:
                far.append(piece)
                if pair == 2:
                    far.append(flip(piece))
            far_sum = project(far, query_grads, chunk, far_sum)

    raw = []
    sources = []
    for number in range(inp_size):
        by, other = divmod(number, pair)
        source = (me - pair * by + inp_size) % inp_size
        source = source ^ other if pair == 2 else source
        sources.append(source)
        block = lax.dynamic_slice_in_dim(gathered, source * shard, shard, axis=1)
        held = near_sum if by == 0 else far_sum
        first = number if by == 0 else number - pair
        rows = held[:, first * blocks * shard:(first + 1) * blocks * shard].reshape(queries, blocks, shard, width)
        raw.append(jnp.sum(rows * block.astype(jnp.float32)[None], axis=3))
    placed = []
    for at in range(inp_size):
        placed.append(sum(jnp.where(source == at, value, 0.0) for source, value in zip(sources, raw)))
    raw = jnp.stack(placed, axis=2).reshape(queries, blocks, tokens)
    raw = xor_sum(xor_sum(raw, "inp", inp_size), "out", out_size)
    equal = token_ids[:, :, None] == token_ids[:, None, :]
    counts = jnp.sum(equal.astype(jnp.int32), axis=2)
    weight = loss_mask.astype(jnp.float32) / counts.astype(jnp.float32)
    return raw * weight[None]


def solution(mesh):
    in_specs = (
        P("grp", "out", "inp"),
        P("grp", "inp", "out"),
        P(None, "out", "inp"),
        P("grp", None),
        P("grp", None),
    )
    out_specs = P(None, "grp", None)
    body = functools.partial(shards, mesh.shape["inp"], mesh.shape["out"])
    return jax.shard_map(body, mesh=mesh, in_specs=in_specs, out_specs=out_specs, check_vma=False)
```

```python
import functools

import jax
import jax.numpy as jnp
from jax import lax
from jax.experimental import pallas as pl
from jax.experimental.pallas import tpu as pltpu
from jax.sharding import PartitionSpec as P

WEIGHTS = (8, 8, 6, 3, 3)
GROUPS = (2, 2, 1)
HELPER_VMEM = 1024 * 1024


def tile_of(length, most):
    size = min(length, most)
    while length % size:
        size -= 128
    return size


def project_kernel(parts, begin, query, fresh, keep, passes, tile, *refs):
    g_refs, q_ref = refs[:parts], refs[parts]
    if keep:
        sum_ref, mark_ref, x_ref, sems = refs[-4:]
    elif parts == 1:
        x_ref, (sum_ref, mark_ref) = g_refs[0], refs[-2:]
    else:
        sum_ref, mark_ref, x_ref, sems = refs[-4:]
    depth = x_ref.shape[1]
    queries, total, width = sum_ref.shape
    copies = []
    if parts > 1:
        rows = g_refs[0].shape[0]
        together = total // rows
        for at, g_ref in enumerate(g_refs):
            row, column = at % together, sum(ref.shape[1] for ref in g_refs[:at // together * together:together])
            where = x_ref.at[pl.ds(row * rows, rows), pl.ds(column, g_ref.shape[1])]
            copies.append(pltpu.make_async_copy(g_ref, where, sems.at[at]))
    for copy in copies:
        copy.start()
    mark_ref[...] = jnp.zeros_like(mark_ref)
    part = depth // passes

    def step(block_ref):
        number, at, turn = pl.program_id(0), pl.program_id(1), pl.program_id(2)

        if copies:

            @pl.when((number == 0) & (at == 0) & (turn == 0))
            def _():
                for copy in copies:
                    copy.wait()

        columns = pl.ds(pl.multiple_of(turn * part, part), part)
        product = jnp.dot(x_ref[:, columns], block_ref[0], preferred_element_type=jnp.float32)
        where = (number, slice(None), pl.ds(pl.multiple_of(at * tile, tile), tile))
        if not fresh:
            sum_ref[where] += product
        elif passes == 1:
            sum_ref[where] = product
        else:

            @pl.when(turn == 0)
            def _():
                sum_ref[where] = product

            @pl.when(turn > 0)
            def _():
                sum_ref[where] += product

    pltpu.emit_pipeline(
        step,
        grid=(queries, width // tile, passes),
        in_specs=[pl.BlockSpec((1, part, tile), lambda q, i, k: (q, k, i))],
    )(q_ref.at[pl.ds(query, queries), pl.ds(begin, depth), :])


def project(spans, query_grads, begin, query, queries, running, passes, tile, others=(), keep=False):
    parts = [part for span in spans for part in span]
    rows = parts[0].shape[0]
    depth = sum(span[0].shape[1] for span in spans)
    width = query_grads.shape[2]
    total = rows * len(spans[0])
    fresh = running is None
    laid = len(parts) == 1
    any_spec = pl.BlockSpec(memory_space=pl.ANY)
    vmem_spec = pl.BlockSpec(memory_space=pltpu.VMEM)
    out_shape = [
        jax.ShapeDtypeStruct((queries, total, width), jnp.float32),
        jax.ShapeDtypeStruct((8, 128), jnp.float32),
    ]
    if keep:
        out_shape.append(jax.ShapeDtypeStruct((total, depth), jnp.bfloat16))
    scratch = [] if laid or keep else [pltpu.VMEM((total, depth), jnp.bfloat16)]
    if not laid:
        scratch.append(pltpu.SemaphoreType.DMA((len(parts),)))
    return pl.pallas_call(
        functools.partial(project_kernel, len(parts), begin, query, fresh, keep, passes, tile_of(width, tile)),
        in_specs=[vmem_spec if laid else any_spec] * len(parts)
        + [any_spec, any_spec if fresh else vmem_spec]
        + [any_spec] * len(others),
        out_specs=[vmem_spec] * len(out_shape),
        out_shape=out_shape,
        scratch_shapes=scratch,
        input_output_aliases={} if fresh else {len(parts) + 1: 0},
        cost_estimate=pl.CostEstimate(flops=1024, bytes_accessed=1024, transcendentals=0),
        compiler_params=pltpu.CompilerParams(vmem_limit_bytes=26 * 1024 * 1024),
        name="project",
    )(*parts, query_grads, query_grads if fresh else running, *others)


def score_kernel(inp_size, pair, queries, ring, *refs):
    near_refs, refs = refs[:queries], refs[queries:]
    if inp_size > pair:
        far_ref, refs = refs[0], refs[1:]
    *a_refs, out_ref, held, sems = refs
    blocks, shard, width = held.shape[1:]
    me, here = lax.axis_index("inp"), lax.axis_index("out")
    sources = []
    for number in range(inp_size):
        by, other = divmod(number, pair)
        source = lax.rem(me - pair * by + inp_size, inp_size)
        sources.append(jnp.bitwise_xor(source, other) if pair == 2 else source)
    for number, source in enumerate(sources):
        if len(a_refs) == 1:
            begin = pl.multiple_of(source * shard, shard)
            pltpu.make_async_copy(
                a_refs[0].at[:, pl.ds(begin, shard), :], held.at[number], sems.at[number]
            ).start()
            continue
        for at, a_ref in enumerate(a_refs):
            for place, spot in enumerate(ring):

                @pl.when((here == spot) & (source == ring[place - at]))
                def _(a_ref=a_ref, number=number):
                    pltpu.make_async_copy(a_ref, held.at[number], sems.at[number]).start()

    lanes = 128
    for number, source in enumerate(sources):
        pltpu.make_async_copy(held.at[number], held.at[number], sems.at[number]).wait()
        for query in range(queries):
            total = None
            for at in range(0, width, lanes):
                block = held[number, :, :, at:at + lanes].reshape(blocks * shard, lanes).astype(jnp.float32)
                begin = (number if number < pair else number - pair) * blocks * shard
                where = (query, slice(begin, begin + blocks * shard), slice(at, at + lanes))
                rows = near_refs[query][(0, *where[1:])] if number < pair else far_ref[where]
                term = rows * block
                total = term if total is None else total + term
            out_ref[source, query, :] = jnp.sum(total.T, axis=0)


def score(sums, slots, ring, inp_size, pair, queries, blocks, shard):
    width = sums[0].shape[2]
    return pl.pallas_call(
        functools.partial(score_kernel, inp_size, pair, queries, ring),
        in_specs=[pl.BlockSpec(memory_space=pltpu.VMEM)] * len(sums)
        + [pl.BlockSpec(memory_space=pl.ANY)] * len(slots),
        out_specs=pl.BlockSpec(memory_space=pltpu.VMEM),
        out_shape=jax.ShapeDtypeStruct((inp_size, queries, blocks * shard), jnp.float32),
        scratch_shapes=[
            pltpu.VMEM((inp_size, blocks, shard, width), jnp.bfloat16),
            pltpu.SemaphoreType.DMA((inp_size,)),
        ],
        compiler_params=pltpu.CompilerParams(vmem_limit_bytes=10 * 1024 * 1024),
        name="score",
    )(*sums, *slots)


def xor_sum(value, axis, size):
    if size & (size - 1):
        return lax.psum(value, axis)
    terms = [value]
    for other in range(1, size):
        terms.append(lax.ppermute(value, axis, [(at, at ^ other) for at in range(size)]))
    while len(terms) > 1:
        terms = [terms[at] + terms[at + 1] for at in range(0, len(terms), 2)]
    return terms[0]


def after(value, *others):
    any_spec = pl.BlockSpec(memory_space=pl.ANY)
    return pl.pallas_call(
        lambda *refs: None,
        in_specs=[any_spec] * (1 + len(others)),
        out_specs=any_spec,
        out_shape=jax.ShapeDtypeStruct(value.shape, value.dtype),
        input_output_aliases={0: 0},
        compiler_params=pltpu.CompilerParams(vmem_limit_bytes=HELPER_VMEM),
        name="after",
    )(pltpu.with_memory_space_constraint(value, pltpu.VMEM), *others)


def in_hbm(value):
    return pltpu.with_memory_space_constraint(value, pltpu.HBM)


def cut_kernel(spans, source_ref, *refs):
    copies = []
    for at, (begin, length) in enumerate(spans):
        copies.append(pltpu.make_async_copy(source_ref.at[:, pl.ds(begin, length)], refs[at], refs[-1].at[at]))
    for copy in copies:
        copy.start()
    for copy in copies:
        copy.wait()


def cut(source, spans):
    return pl.pallas_call(
        functools.partial(cut_kernel, spans),
        in_specs=[pl.BlockSpec(memory_space=pl.ANY)],
        out_specs=[pl.BlockSpec(memory_space=pltpu.VMEM)] * len(spans),
        out_shape=[jax.ShapeDtypeStruct((source.shape[0], length), source.dtype) for _, length in spans],
        scratch_shapes=[pltpu.SemaphoreType.DMA((len(spans),))],
        compiler_params=pltpu.CompilerParams(vmem_limit_bytes=HELPER_VMEM),
        name="cut",
    )(source)


def shards(inp_size, out_size, activations, out_grads, query_grads, token_ids, loss_mask):
    blocks, shard, depth = out_grads.shape
    queries, _, width = query_grads.shape
    tokens = token_ids.shape[1]
    pair = 2 if inp_size % 2 == 0 else 1
    chips = inp_size // pair
    rows = blocks * shard

    unit = 256 if depth % 256 == 0 else depth
    units = depth // unit
    edges = [0]
    for at in range(len(WEIGHTS)):
        edges.append(units * sum(WEIGHTS[:at + 1]) // sum(WEIGHTS) * unit)
    spans = [(begin, end - begin) for begin, end in zip(edges, edges[1:]) if end > begin]
    chunks = len(spans)

    def flip(value):
        return lax.ppermute(value, "inp", [(at, at ^ 1) for at in range(inp_size)])

    def shift(value, by):
        return lax.ppermute(value, "inp", [(at, (at + pair * by) % inp_size) for at in range(inp_size)])

    own = in_hbm(out_grads.reshape(rows, depth))
    near = [own] + ([pltpu.with_memory_space_constraint(flip(own), pltpu.VMEM)] if pair == 2 else [])
    query_grads = in_hbm(query_grads)
    activations = in_hbm(activations)
    line = inp_size == out_size and activations.shape[1] == shard
    ring = list(range(0, out_size, 2)) + list(range(1, out_size, 2))[::-1]
    turn = [(ring[at - 1], ring[at]) for at in range(out_size)]
    slots = [activations]
    if not line:
        slots = [lax.all_gather(activations, "out", axis=1, tiled=True)]
    elif out_size > 1:
        slots.append(lax.ppermute(activations, "out", turn))

    pieces_out = cut(own, spans) if chips > 1 else []

    def send(chunk):
        return [shift(pieces_out[chunk], by) for by in range(1, chips)]

    settled = [1]

    def step_along(mark):
        if not line or settled[0] == out_size:
            return []
        settled[0] += 1
        slots[-1] = after(slots[-1], mark)
        if len(slots) < out_size:
            slots.append(lax.ppermute(slots[-1], "out", turn))
            return [slots[-2]]
        return [slots[-1]]

    coming = [send(chunk) for chunk in range(chunks)] if chips > 1 else []
    waiting = []

    def receive(mark, count=1):
        pieces = []
        for _ in range(min(count, len(coming))):
            arrived = [after(piece, mark) for piece in coming.pop(0)]
            waiting.append(sum([[piece, flip(piece)] if pair == 2 else [piece] for piece in arrived], []))
            pieces += arrived
        return pieces

    sums = []
    held = near
    for query in range(queries):
        others = []
        if query > 0:
            others = receive(mark) + (step_along(mark) if query == 1 else [])
        near_sum, mark, *kept = project([held], query_grads, 0, query, 1, None, 1, 512, others, len(held) > 1)
        held = kept or [after(held[0], mark)]
        sums.append(near_sum)
    running = None
    done = 0
    counts = list(GROUPS)
    while coming or waiting:
        count = counts.pop(0) if counts else len(coming)
        others = receive(mark, count - len(waiting)) + step_along(mark)
        depth_now = sum(length for _, length in spans[done:done + len(waiting)])
        running, mark = project(
            waiting, query_grads, spans[done][0], 0, queries, running, 1, 2048 if depth_now <= 1024 else 1024, others
        )
        done += len(waiting)
        waiting.clear()
    if running is not None:
        sums.append(running)
    raw = score(sums, slots, ring, inp_size, pair, queries, blocks, shard)
    raw = raw.reshape(inp_size, queries, blocks, shard).transpose(1, 2, 0, 3).reshape(queries, blocks, tokens)
    raw = xor_sum(xor_sum(raw, "inp", inp_size), "out", out_size)
    equal = token_ids[:, :, None] == token_ids[:, None, :]
    counts = jnp.sum(equal.astype(jnp.int32), axis=2)
    weight = loss_mask.astype(jnp.float32) / counts.astype(jnp.float32)
    return raw * weight[None]


def solution(mesh):
    in_specs = (
        P("grp", "out", "inp"),
        P("grp", "inp", "out"),
        P(None, "out", "inp"),
        P("grp", None),
        P("grp", None),
    )
    out_specs = P(None, "grp", None)
    body = functools.partial(shards, mesh.shape["inp"], mesh.shape["out"])
    return jax.shard_map(body, mesh=mesh, in_specs=in_specs, out_specs=out_specs, check_vma=False)
```

```python
import functools
import typing

import jax
import jax.numpy as jnp
from jax import lax
from jax.experimental import pallas as pl
from jax.experimental.pallas import tpu as pltpu
from jax.sharding import PartitionSpec as P

WEIGHTS = (8, 7, 8, 5)
GROUPS = (2, 1, 1)
HELPER_VMEM = 1024 * 1024
TILE = 512
STRIP_ROWS = 8192


def tile_of(length, most):
    size = min(length, most)
    while length % size:
        size -= 128
    return size


class Plan(typing.NamedTuple):
    query: int
    queries: int
    begin: int
    depth: int
    tile: int
    strips: int
    turns: int

    @property
    def steps(self):
        return self.queries * self.turns


def plan_of(query, queries, begin, depth, width, room):
    tile = tile_of(width, TILE)
    strips = 1
    while strips * 2 * depth <= room and width // tile % (strips * 2) == 0:
        strips *= 2
    return Plan(query, queries, begin, depth, tile, strips, width // tile // strips)


def fetches(plan, step, q_ref, slot_ref, sems):
    number, turn = plan.query + step // plan.turns, step % plan.turns
    copies = []
    for strip in range(plan.strips):
        column = (turn * plan.strips + strip) * plan.tile
        if not isinstance(column, int):
            column = pl.multiple_of(column, plan.tile)
        source = q_ref.at[number, pl.ds(plan.begin, plan.depth), pl.ds(column, plan.tile)]
        target = slot_ref.at[pl.ds(strip * plan.depth, plan.depth)]
        copies.append(pltpu.make_async_copy(source, target, sems.at[strip]))
    return copies


def run(copies, start):
    for copy in copies:
        if start:
            copy.start()
        else:
            copy.wait()


def load_kernel(plan, source_ref, q_ref, slot_ref, x_ref, sem, sems):
    first = fetches(plan, 0, q_ref, slot_ref, sems)
    rows = pltpu.make_async_copy(source_ref, x_ref.at[pl.ds(0, source_ref.shape[0])], sem)
    run(first, True)
    rows.start()
    run(first, False)
    rows.wait()


def load(own, total, query_grads, plan, room):
    vmem_spec = pl.BlockSpec(memory_space=pltpu.VMEM)
    return pl.pallas_call(
        functools.partial(load_kernel, plan),
        in_specs=[pl.BlockSpec(memory_space=pl.ANY)] * 2,
        out_specs=[vmem_spec] * 2,
        out_shape=[
            jax.ShapeDtypeStruct((room, plan.tile), jnp.bfloat16),
            jax.ShapeDtypeStruct((total, own.shape[1]), jnp.bfloat16),
        ],
        scratch_shapes=[pltpu.SemaphoreType.DMA, pltpu.SemaphoreType.DMA((plan.strips,))],
        cost_estimate=pl.CostEstimate(flops=1024, bytes_accessed=1024, transcendentals=0),
        compiler_params=pltpu.CompilerParams(vmem_limit_bytes=HELPER_VMEM),
        name="load",
    )(own, query_grads)


def project_kernel(parts, plan, later, fresh, laid, *refs):
    g_refs, q_ref = refs[:parts], refs[parts]
    sum_ref, mark_ref, slot_a, x_ref, slot_b, sems, sems_a, sems_b = refs[-8:]
    total = x_ref.shape[0]
    copies = []
    together = total // g_refs[0].shape[0] if parts and not laid else 1
    column = 0
    for at, g_ref in enumerate(g_refs):
        rows = g_ref.shape[0]
        row = total - rows if laid else at % together * rows
        where = x_ref.at[pl.ds(row, rows), pl.ds(column, g_ref.shape[1])]
        copies.append(pltpu.make_async_copy(g_ref, where, sems.at[at]))
        if not laid and at % together == together - 1:
            column += g_ref.shape[1]
    steps = plan.steps
    run(copies, True)
    if steps > 1:
        run(fetches(plan, 1, q_ref, slot_b, sems_b), True)
    mark_ref[...] = jnp.zeros_like(mark_ref)
    run(copies, False)

    def multiply(step, slot_ref):
        number, turn = step // plan.turns, step % plan.turns
        for strip in range(plan.strips):
            product = jnp.dot(
                x_ref[...],
                slot_ref[strip * plan.depth:(strip + 1) * plan.depth, :],
                preferred_element_type=jnp.float32,
            )
            begin = (turn * plan.strips + strip) * plan.tile
            if not isinstance(begin, int):
                begin = pl.multiple_of(begin, plan.tile)
            where = (number, slice(None), pl.ds(begin, plan.tile))
            if fresh:
                sum_ref[where] = product
            else:
                sum_ref[where] += product

    def both(pair):
        step = pair * 2

        @pl.when(pair > 0)
        def _():
            run(fetches(plan, step + 1, q_ref, slot_b, sems_b), True)
            run(fetches(plan, step, q_ref, slot_a, sems_a), False)

        multiply(step, slot_a)

        @pl.when(step + 2 < steps)
        def _():
            run(fetches(plan, step + 2, q_ref, slot_a, sems_a), True)

        if later is not None:

            @pl.when(step + 2 >= steps)
            def _():
                run(fetches(later, 0, q_ref, slot_a, sems_a), True)

        run(fetches(plan, step + 1, q_ref, slot_b, sems_b), False)
        multiply(step + 1, slot_b)

    if steps % 2 == 0:

        @pl.loop(0, steps // 2)
        def _(pair):
            both(pair)
    else:
        for step in range(steps):
            slot_ref, slot_sems = (slot_a, sems_a) if step % 2 == 0 else (slot_b, sems_b)
            if step > 0:
                run(fetches(plan, step, q_ref, slot_ref, slot_sems), step > 1)
                if step > 1:
                    run(fetches(plan, step, q_ref, slot_ref, slot_sems), False)
            multiply(step, slot_ref)
        if later is not None:
            run(fetches(later, 0, q_ref, slot_a, sems_a), True)
    if later is not None:
        run(fetches(later, 0, q_ref, slot_a, sems_a), False)


def project(parts, rows, query_grads, plan, later, slot, running, others=(), laid=None):
    width = query_grads.shape[2]
    fresh = running is None
    any_spec = pl.BlockSpec(memory_space=pl.ANY)
    vmem_spec = pl.BlockSpec(memory_space=pltpu.VMEM)
    operands = [*parts, query_grads, slot]
    in_specs = [any_spec] * (len(parts) + 1) + [vmem_spec]
    aliases = {len(parts) + 1: 2}
    if not fresh:
        aliases[len(operands)] = 0
        operands.append(running)
        in_specs.append(vmem_spec)
    out_shape = [
        jax.ShapeDtypeStruct((plan.queries, rows, width), jnp.float32),
        jax.ShapeDtypeStruct((8, 128), jnp.float32),
        jax.ShapeDtypeStruct(slot.shape, slot.dtype),
    ]
    scratch = []
    if laid is not None:
        aliases[len(operands)] = 3
        operands.append(laid)
        in_specs.append(vmem_spec)
        out_shape.append(jax.ShapeDtypeStruct(laid.shape, laid.dtype))
    else:
        scratch.append(pltpu.VMEM((rows, plan.depth), jnp.bfloat16))
    scratch += [
        pltpu.VMEM(slot.shape, slot.dtype),
        pltpu.SemaphoreType.DMA((max(len(parts), 1),)),
        pltpu.SemaphoreType.DMA((max(plan.strips, later.strips if later else 1),)),
        pltpu.SemaphoreType.DMA((plan.strips,)),
    ]
    limit = 2 * slot.size + (2 * rows * plan.depth if laid is None else 0) + 4 * 1024 * 1024
    return pl.pallas_call(
        functools.partial(project_kernel, len(parts), plan, later, fresh, laid is not None),
        in_specs=in_specs + [any_spec] * len(others),
        out_specs=[vmem_spec] * len(out_shape),
        out_shape=out_shape,
        scratch_shapes=scratch,
        input_output_aliases=aliases,
        cost_estimate=pl.CostEstimate(flops=1024, bytes_accessed=1024, transcendentals=0),
        compiler_params=pltpu.CompilerParams(vmem_limit_bytes=limit),
        name="project",
    )(*operands, *others)


def score_kernel(inp_size, pair, queries, ring, *refs):
    near_refs, refs = refs[:queries], refs[queries:]
    if inp_size > pair:
        far_ref, refs = refs[0], refs[1:]
    *a_refs, out_ref, held, sems = refs
    blocks, shard, width = held.shape[1:]
    me, here = lax.axis_index("inp"), lax.axis_index("out")
    sources = []
    for number in range(inp_size):
        by, other = divmod(number, pair)
        source = lax.rem(me - pair * by + inp_size, inp_size)
        sources.append(jnp.bitwise_xor(source, other) if pair == 2 else source)
    for number, source in enumerate(sources):
        if len(a_refs) == 1:
            begin = pl.multiple_of(source * shard, shard)
            pltpu.make_async_copy(
                a_refs[0].at[:, pl.ds(begin, shard), :], held.at[number], sems.at[number]
            ).start()
            continue
        for at, a_ref in enumerate(a_refs):
            for place, spot in enumerate(ring):

                @pl.when((here == spot) & (source == ring[place - at]))
                def _(a_ref=a_ref, number=number):
                    pltpu.make_async_copy(a_ref, held.at[number], sems.at[number]).start()

    lanes = 128
    for number, source in enumerate(sources):
        pltpu.make_async_copy(held.at[number], held.at[number], sems.at[number]).wait()
        for query in range(queries):
            total = None
            for at in range(0, width, lanes):
                block = held[number, :, :, at:at + lanes].reshape(blocks * shard, lanes).astype(jnp.float32)
                begin = (number if number < pair else number - pair) * blocks * shard
                where = (query, slice(begin, begin + blocks * shard), slice(at, at + lanes))
                rows = near_refs[query][(0, *where[1:])] if number < pair else far_ref[where]
                term = rows * block
                total = term if total is None else total + term
            out_ref[source, query, :] = jnp.sum(total.T, axis=0)


def score(sums, slots, ring, inp_size, pair, queries, blocks, shard):
    width = sums[0].shape[2]
    return pl.pallas_call(
        functools.partial(score_kernel, inp_size, pair, queries, ring),
        in_specs=[pl.BlockSpec(memory_space=pltpu.VMEM)] * len(sums)
        + [pl.BlockSpec(memory_space=pl.ANY)] * len(slots),
        out_specs=pl.BlockSpec(memory_space=pltpu.VMEM),
        out_shape=jax.ShapeDtypeStruct((inp_size, queries, blocks * shard), jnp.float32),
        scratch_shapes=[
            pltpu.VMEM((inp_size, blocks, shard, width), jnp.bfloat16),
            pltpu.SemaphoreType.DMA((inp_size,)),
        ],
        compiler_params=pltpu.CompilerParams(vmem_limit_bytes=6 * 1024 * 1024),
        name="score",
    )(*sums, *slots)


def xor_sum(value, axis, size):
    if size & (size - 1):
        return lax.psum(value, axis)
    terms = [value]
    for other in range(1, size):
        terms.append(lax.ppermute(value, axis, [(at, at ^ other) for at in range(size)]))
    while len(terms) > 1:
        terms = [terms[at] + terms[at + 1] for at in range(0, len(terms), 2)]
    return terms[0]


def after(value, *others):
    any_spec = pl.BlockSpec(memory_space=pl.ANY)
    return pl.pallas_call(
        lambda *refs: None,
        in_specs=[any_spec] * (1 + len(others)),
        out_specs=any_spec,
        out_shape=jax.ShapeDtypeStruct(value.shape, value.dtype),
        input_output_aliases={0: 0},
        compiler_params=pltpu.CompilerParams(vmem_limit_bytes=HELPER_VMEM),
        name="after",
    )(pltpu.with_memory_space_constraint(value, pltpu.VMEM), *others)


def in_hbm(value):
    return pltpu.with_memory_space_constraint(value, pltpu.HBM)


def cut_kernel(spans, source_ref, *refs):
    outs, sems = refs[:-1], refs[-1]
    copies = []
    for at, (span, out_ref) in enumerate(zip(spans, outs)):
        copies.append(pltpu.make_async_copy(source_ref.at[:, pl.ds(*span)], out_ref, sems.at[at]))
    run(copies, True)
    run(copies, False)


def cut(source, spans):
    return pl.pallas_call(
        functools.partial(cut_kernel, spans),
        in_specs=[pl.BlockSpec(memory_space=pl.ANY)],
        out_specs=[pl.BlockSpec(memory_space=pltpu.VMEM)] * len(spans),
        out_shape=[jax.ShapeDtypeStruct((source.shape[0], length), source.dtype) for _, length in spans],
        scratch_shapes=[pltpu.SemaphoreType.DMA((len(spans),))],
        compiler_params=pltpu.CompilerParams(vmem_limit_bytes=HELPER_VMEM),
        name="cut",
    )(source)


def shards(inp_size, out_size, activations, out_grads, query_grads, token_ids, loss_mask):
    blocks, shard, depth = out_grads.shape
    queries, _, width = query_grads.shape
    tokens = token_ids.shape[1]
    pair = 2 if inp_size % 2 == 0 else 1
    chips = inp_size // pair
    rows = blocks * shard

    unit = 256 if depth % 256 == 0 else depth
    units = depth // unit
    edges = [0]
    for at in range(len(WEIGHTS)):
        edges.append(units * sum(WEIGHTS[:at + 1]) // sum(WEIGHTS) * unit)
    spans = [(begin, end - begin) for begin, end in zip(edges, edges[1:]) if end > begin]
    chunks = len(spans)

    def flip(value):
        return lax.ppermute(value, "inp", [(at, at ^ 1) for at in range(inp_size)])

    def shift(value, by):
        return lax.ppermute(value, "inp", [(at, (at + pair * by) % inp_size) for at in range(inp_size)])

    own = in_hbm(out_grads.reshape(rows, depth))
    near = [pltpu.with_memory_space_constraint(flip(own), pltpu.VMEM)] if pair == 2 else []
    query_grads = in_hbm(query_grads)
    activations = in_hbm(activations)
    line = inp_size == out_size and activations.shape[1] == shard and out_size > 1
    ring = list(range(0, out_size, 2)) + list(range(1, out_size, 2))[::-1]
    turn = [(ring[at - 1], ring[at]) for at in range(out_size)]
    pieces_out = cut(own, spans) if chips > 1 else []

    slots = [activations]
    if line:
        slots.append(lax.ppermute(activations, "out", turn))
    else:
        slots = [lax.all_gather(activations, "out", axis=1, tiled=True)]

    def step_along(mark):
        if not line or len(slots) == out_size:
            return []
        slots[-1] = ended = after(slots[-1], mark)
        slots.append(lax.ppermute(ended, "out", turn))
        return [ended]

    coming = []
    if chips > 1:
        coming = [[shift(piece, by) for by in range(1, chips)] for piece in pieces_out]
    waiting = []

    def receive(mark, count=1):
        pieces = []
        for _ in range(min(count, len(coming))):
            arrived = [after(piece, mark) for piece in coming.pop(0)]
            waiting.extend(sum([[piece, flip(piece)] if pair == 2 else [piece] for piece in arrived], []))
            pieces += arrived
        return pieces

    room = max(depth, STRIP_ROWS if depth >= STRIP_ROWS // 2 else 0)
    plans = [plan_of(query, 1, 0, depth, width, depth) for query in range(queries)]
    chosen = []
    for count in GROUPS + (1,) * chunks:
        group, spans = (spans[:count], spans[count:]) if chips > 1 else ([], [])
        if group:
            chosen.append(count)
            length = sum(length for _, length in group)
            plans.append(plan_of(0, queries, group[0][0], length, width, room))
    plans.append(None)

    slot, laid = load(own, pair * rows, query_grads, plans[0], room)
    sums = []
    mark = None
    for query in range(queries):
        others = []
        if query > 0:
            others = receive(mark) + step_along(mark)
        near_sum, mark, slot, laid = project(
            near if query == 0 else [], pair * rows, query_grads, plans[query], plans[query + 1], slot, None, others, laid
        )
        sums.append(near_sum)
    running = None
    got = min(queries - 1, len(coming))
    for at, count in enumerate(chosen):
        others = receive(mark, count - (got if at == 0 else 0)) + (step_along(mark) if at > 0 else [])
        running, mark, slot = project(
            waiting, (inp_size - pair) * rows, query_grads, plans[queries + at], plans[queries + at + 1], slot, running, others
        )
        waiting.clear()
    if running is not None:
        sums.append(running)
    raw = score(sums, slots, ring, inp_size, pair, queries, blocks, shard)
    raw = raw.reshape(inp_size, queries, blocks, shard).transpose(1, 2, 0, 3).reshape(queries, blocks, tokens)
    raw = xor_sum(xor_sum(raw, "inp", inp_size), "out", out_size)
    equal = token_ids[:, :, None] == token_ids[:, None, :]
    counts = jnp.sum(equal.astype(jnp.int32), axis=2)
    weight = loss_mask.astype(jnp.float32) / counts.astype(jnp.float32)
    return raw * weight[None]


def solution(mesh):
    in_specs = (
        P("grp", "out", "inp"),
        P("grp", "inp", "out"),
        P(None, "out", "inp"),
        P("grp", None),
        P("grp", None),
    )
    out_specs = P(None, "grp", None)
    body = functools.partial(shards, mesh.shape["inp"], mesh.shape["out"])
    return jax.shard_map(body, mesh=mesh, in_specs=in_specs, out_specs=out_specs, check_vma=False)
```

```python
import functools
import typing

import jax
import jax.numpy as jnp
from jax import lax
from jax.experimental import pallas as pl
from jax.experimental.pallas import tpu as pltpu
from jax.sharding import PartitionSpec as P

WEIGHTS = (8, 6, 8, 6)
GROUPS = (2, 1, 1)
HELPER_VMEM = 1024 * 1024
TILE = 512
STRIP_ROWS = 8192


def tile_of(length, most):
    size = min(length, most)
    while length % size:
        size -= 128
    return size


class Plan(typing.NamedTuple):
    query: int
    queries: int
    begin: int
    depth: int
    tile: int
    strips: int
    turns: int

    @property
    def steps(self):
        return self.queries * self.turns


def plan_of(query, queries, begin, depth, width, room):
    tile = tile_of(width, TILE)
    strips = 1
    while strips * 2 * depth <= room and width // tile % (strips * 2) == 0:
        strips *= 2
    return Plan(query, queries, begin, depth, tile, strips, width // tile // strips)


def fetches(plan, step, q_ref, slot_ref, sems):
    number, turn = plan.query + step // plan.turns, step % plan.turns
    copies = []
    for strip in range(plan.strips):
        column = (turn * plan.strips + strip) * plan.tile
        if not isinstance(column, int):
            column = pl.multiple_of(column, plan.tile)
        source = q_ref.at[number, pl.ds(plan.begin, plan.depth), pl.ds(column, plan.tile)]
        target = slot_ref.at[pl.ds(strip * plan.depth, plan.depth)]
        copies.append(pltpu.make_async_copy(source, target, sems.at[strip]))
    return copies


def run(copies, start):
    for copy in copies:
        if start:
            copy.start()
        else:
            copy.wait()


def load_kernel(plan, parts, *refs):
    g_refs, (q_ref, slot_ref, x_ref, sems, slot_sems) = refs[:parts], refs[parts:]
    copies = fetches(plan, 0, q_ref, slot_ref, slot_sems)
    column = 0
    for at, g_ref in enumerate(g_refs):
        rows, columns = g_ref.shape
        where = x_ref.at[pl.ds(0, rows), pl.ds(column, columns)]
        copies.append(pltpu.make_async_copy(g_ref, where, sems.at[at]))
        column += columns
    run(copies, True)
    run(copies, False)


def load(own, total, query_grads, plan, room):
    vmem_spec = pl.BlockSpec(memory_space=pltpu.VMEM)
    depth = sum(part.shape[1] for part in own)
    return pl.pallas_call(
        functools.partial(load_kernel, plan, len(own)),
        in_specs=[pl.BlockSpec(memory_space=pl.ANY)] * (len(own) + 1),
        out_specs=[vmem_spec] * 2,
        out_shape=[
            jax.ShapeDtypeStruct((room, plan.tile), jnp.bfloat16),
            jax.ShapeDtypeStruct((total, depth), jnp.bfloat16),
        ],
        scratch_shapes=[pltpu.SemaphoreType.DMA((len(own),)), pltpu.SemaphoreType.DMA((plan.strips,))],
        cost_estimate=pl.CostEstimate(flops=1024, bytes_accessed=1024, transcendentals=0),
        compiler_params=pltpu.CompilerParams(vmem_limit_bytes=HELPER_VMEM),
        name="load",
    )(*own, query_grads)


def project_kernel(parts, plan, later, fresh, laid, *refs):
    g_refs, q_ref = refs[:parts], refs[parts]
    sum_ref, mark_ref, slot_a, x_ref, slot_b, sems, sems_a, sems_b = refs[-8:]
    total = x_ref.shape[0]
    copies = []
    together = total // g_refs[0].shape[0] if parts and not laid else 1
    column = 0
    for at, g_ref in enumerate(g_refs):
        rows = g_ref.shape[0]
        row = total - rows if laid else at % together * rows
        where = x_ref.at[pl.ds(row, rows), pl.ds(column, g_ref.shape[1])]
        copies.append(pltpu.make_async_copy(g_ref, where, sems.at[at]))
        if not laid and at % together == together - 1:
            column += g_ref.shape[1]
    steps = plan.steps
    run(copies, True)
    if steps > 1:
        run(fetches(plan, 1, q_ref, slot_b, sems_b), True)
    mark_ref[...] = jnp.zeros_like(mark_ref)
    run(copies, False)

    def multiply(step, slot_ref):
        number, turn = step // plan.turns, step % plan.turns
        for strip in range(plan.strips):
            product = jnp.dot(
                x_ref[...],
                slot_ref[strip * plan.depth:(strip + 1) * plan.depth, :],
                preferred_element_type=jnp.float32,
            )
            begin = (turn * plan.strips + strip) * plan.tile
            if not isinstance(begin, int):
                begin = pl.multiple_of(begin, plan.tile)
            where = (number, slice(None), pl.ds(begin, plan.tile))
            if fresh:
                sum_ref[where] = product
            else:
                sum_ref[where] += product

    def both(pair):
        step = pair * 2

        @pl.when(pair > 0)
        def _():
            run(fetches(plan, step + 1, q_ref, slot_b, sems_b), True)
            run(fetches(plan, step, q_ref, slot_a, sems_a), False)

        multiply(step, slot_a)

        @pl.when(step + 2 < steps)
        def _():
            run(fetches(plan, step + 2, q_ref, slot_a, sems_a), True)

        if later is not None:

            @pl.when(step + 2 >= steps)
            def _():
                run(fetches(later, 0, q_ref, slot_a, sems_a), True)

        run(fetches(plan, step + 1, q_ref, slot_b, sems_b), False)
        multiply(step + 1, slot_b)

    if steps % 2 == 0:

        @pl.loop(0, steps // 2)
        def _(pair):
            both(pair)
    else:
        for step in range(steps):
            slot_ref, slot_sems = (slot_a, sems_a) if step % 2 == 0 else (slot_b, sems_b)
            if step > 0:
                run(fetches(plan, step, q_ref, slot_ref, slot_sems), step > 1)
                if step > 1:
                    run(fetches(plan, step, q_ref, slot_ref, slot_sems), False)
            multiply(step, slot_ref)
        if later is not None:
            run(fetches(later, 0, q_ref, slot_a, sems_a), True)
    if later is not None:
        run(fetches(later, 0, q_ref, slot_a, sems_a), False)


def project(parts, rows, query_grads, plan, later, slot, running, others=(), laid=None):
    width = query_grads.shape[2]
    fresh = running is None
    any_spec = pl.BlockSpec(memory_space=pl.ANY)
    vmem_spec = pl.BlockSpec(memory_space=pltpu.VMEM)
    operands = [*parts, query_grads, slot]
    in_specs = [any_spec] * (len(parts) + 1) + [vmem_spec]
    aliases = {len(parts) + 1: 2}
    if not fresh:
        aliases[len(operands)] = 0
        operands.append(running)
        in_specs.append(vmem_spec)
    out_shape = [
        jax.ShapeDtypeStruct((plan.queries, rows, width), jnp.float32),
        jax.ShapeDtypeStruct((8, 128), jnp.float32),
        jax.ShapeDtypeStruct(slot.shape, slot.dtype),
    ]
    scratch = []
    if laid is not None:
        aliases[len(operands)] = 3
        operands.append(laid)
        in_specs.append(vmem_spec)
        out_shape.append(jax.ShapeDtypeStruct(laid.shape, laid.dtype))
    else:
        scratch.append(pltpu.VMEM((rows, plan.depth), jnp.bfloat16))
    scratch += [
        pltpu.VMEM(slot.shape, slot.dtype),
        pltpu.SemaphoreType.DMA((max(len(parts), 1),)),
        pltpu.SemaphoreType.DMA((max(plan.strips, later.strips if later else 1),)),
        pltpu.SemaphoreType.DMA((plan.strips,)),
    ]
    limit = 2 * slot.size + (2 * rows * plan.depth if laid is None else 0) + 4 * 1024 * 1024
    return pl.pallas_call(
        functools.partial(project_kernel, len(parts), plan, later, fresh, laid is not None),
        in_specs=in_specs + [any_spec] * len(others),
        out_specs=[vmem_spec] * len(out_shape),
        out_shape=out_shape,
        scratch_shapes=scratch,
        input_output_aliases=aliases,
        cost_estimate=pl.CostEstimate(flops=1024, bytes_accessed=1024, transcendentals=0),
        compiler_params=pltpu.CompilerParams(vmem_limit_bytes=limit),
        name="project",
    )(*operands, *others)


def score_kernel(inp_size, pair, queries, ring, *refs):
    near_refs, refs = refs[:queries], refs[queries:]
    if inp_size > pair:
        far_ref, refs = refs[0], refs[1:]
    *a_refs, out_ref, held, sems = refs
    blocks, shard, width = held.shape[1:]
    me, here = lax.axis_index("inp"), lax.axis_index("out")
    sources = []
    for number in range(inp_size):
        by, other = divmod(number, pair)
        source = lax.rem(me - pair * by + inp_size, inp_size)
        sources.append(jnp.bitwise_xor(source, other) if pair == 2 else source)
    for number, source in enumerate(sources):
        if len(a_refs) == 1:
            begin = pl.multiple_of(source * shard, shard)
            pltpu.make_async_copy(
                a_refs[0].at[:, pl.ds(begin, shard), :], held.at[number], sems.at[number]
            ).start()
            continue
        for at, a_ref in enumerate(a_refs):
            for place, spot in enumerate(ring):

                @pl.when((here == spot) & (source == ring[place - at]))
                def _(a_ref=a_ref, number=number):
                    pltpu.make_async_copy(a_ref, held.at[number], sems.at[number]).start()

    lanes = 128
    for number, source in enumerate(sources):
        pltpu.make_async_copy(held.at[number], held.at[number], sems.at[number]).wait()
        totals = [None] * queries
        begin = (number if number < pair else number - pair) * blocks * shard
        for at in range(0, width, lanes):
            block = held[number, :, :, at:at + lanes].reshape(blocks * shard, lanes).astype(jnp.float32)
            for query in range(queries):
                where = (slice(begin, begin + blocks * shard), slice(at, at + lanes))
                rows = near_refs[query][(0, *where)] if number < pair else far_ref[(query, *where)]
                term = rows * block
                totals[query] = term if totals[query] is None else totals[query] + term
        for query in range(queries):
            out_ref[source, query, :] = jnp.sum(totals[query].T, axis=0)


def score(sums, slots, ring, inp_size, pair, queries, blocks, shard):
    width = sums[0].shape[2]
    return pl.pallas_call(
        functools.partial(score_kernel, inp_size, pair, queries, ring),
        in_specs=[pl.BlockSpec(memory_space=pltpu.VMEM)] * len(sums)
        + [pl.BlockSpec(memory_space=pl.ANY)] * len(slots),
        out_specs=pl.BlockSpec(memory_space=pltpu.VMEM),
        out_shape=jax.ShapeDtypeStruct((inp_size, queries, blocks * shard), jnp.float32),
        scratch_shapes=[
            pltpu.VMEM((inp_size, blocks, shard, width), jnp.bfloat16),
            pltpu.SemaphoreType.DMA((inp_size,)),
        ],
        compiler_params=pltpu.CompilerParams(vmem_limit_bytes=6 * 1024 * 1024),
        name="score",
    )(*sums, *slots)


def xor_sum(value, axis, size):
    if size & (size - 1):
        return lax.psum(value, axis)
    terms = [value]
    for other in range(1, size):
        terms.append(lax.ppermute(value, axis, [(at, at ^ other) for at in range(size)]))
    while len(terms) > 1:
        terms = [terms[at] + terms[at + 1] for at in range(0, len(terms), 2)]
    return terms[0]


def after(value, *others):
    any_spec = pl.BlockSpec(memory_space=pl.ANY)
    return pl.pallas_call(
        lambda *refs: None,
        in_specs=[any_spec] * (1 + len(others)),
        out_specs=any_spec,
        out_shape=jax.ShapeDtypeStruct(value.shape, value.dtype),
        input_output_aliases={0: 0},
        compiler_params=pltpu.CompilerParams(vmem_limit_bytes=HELPER_VMEM),
        name="after",
    )(pltpu.with_memory_space_constraint(value, pltpu.VMEM), *others)


def halve_kernel(source_ref, *refs):
    *outs, sems = refs[-3:]
    begin, copies = 0, []
    for at, out_ref in enumerate(outs):
        where = source_ref.at[:, pl.ds(begin, out_ref.shape[1])]
        copies.append(pltpu.make_async_copy(where, out_ref, sems.at[at]))
        begin += out_ref.shape[1]
    run(copies, True)
    run(copies, False)


def halve(value, *others):
    rows, columns = value.shape
    first = columns // 256 * 128 or columns
    if first == columns:
        return [after(value, *others)]
    return pl.pallas_call(
        halve_kernel,
        in_specs=[pl.BlockSpec(memory_space=pl.ANY)] * (1 + len(others)),
        out_specs=[pl.BlockSpec(memory_space=pltpu.VMEM)] * 2,
        out_shape=[jax.ShapeDtypeStruct((rows, part), value.dtype) for part in (first, columns - first)],
        scratch_shapes=[pltpu.SemaphoreType.DMA((2,))],
        cost_estimate=pl.CostEstimate(flops=1024, bytes_accessed=1024, transcendentals=0),
        compiler_params=pltpu.CompilerParams(vmem_limit_bytes=HELPER_VMEM),
        name="halve",
    )(pltpu.with_memory_space_constraint(value, pltpu.VMEM), *others)


def in_hbm(value):
    return pltpu.with_memory_space_constraint(value, pltpu.HBM)


def cut_kernel(spans, source_ref, *refs):
    outs, sems = refs[:-1], refs[-1]
    copies = []
    for at, (span, out_ref) in enumerate(zip(spans, outs)):
        copies.append(pltpu.make_async_copy(source_ref.at[:, pl.ds(*span)], out_ref, sems.at[at]))
    run(copies, True)
    run(copies, False)


def cut(source, spans):
    return pl.pallas_call(
        functools.partial(cut_kernel, spans),
        in_specs=[pl.BlockSpec(memory_space=pl.ANY)],
        out_specs=[pl.BlockSpec(memory_space=pltpu.VMEM)] * len(spans),
        out_shape=[jax.ShapeDtypeStruct((source.shape[0], length), source.dtype) for _, length in spans],
        scratch_shapes=[pltpu.SemaphoreType.DMA((len(spans),))],
        compiler_params=pltpu.CompilerParams(vmem_limit_bytes=HELPER_VMEM),
        name="cut",
    )(source)


def shards(inp_size, out_size, activations, out_grads, query_grads, token_ids, loss_mask):
    blocks, shard, depth = out_grads.shape
    queries, _, width = query_grads.shape
    tokens = token_ids.shape[1]
    pair = 2 if inp_size % 2 == 0 else 1
    chips = inp_size // pair
    rows = blocks * shard

    unit = 256 if depth % 256 == 0 else depth
    units = depth // unit
    edges = [0]
    for at in range(len(WEIGHTS)):
        edges.append(units * sum(WEIGHTS[:at + 1]) // sum(WEIGHTS) * unit)
    spans = [(begin, end - begin) for begin, end in zip(edges, edges[1:]) if end > begin]
    chunks = len(spans)

    def flip(value):
        return lax.ppermute(value, "inp", [(at, at ^ 1) for at in range(inp_size)])

    def shift(value, by):
        return lax.ppermute(value, "inp", [(at, (at + pair * by) % inp_size) for at in range(inp_size)])

    own = in_hbm(out_grads.reshape(rows, depth))
    near = [pltpu.with_memory_space_constraint(flip(own), pltpu.VMEM)] if pair == 2 else []
    query_grads = in_hbm(query_grads)
    activations = in_hbm(activations)
    line = inp_size == out_size and activations.shape[1] == shard and out_size > 1
    ring = list(range(0, out_size, 2)) + list(range(1, out_size, 2))[::-1]
    turn = [(ring[at - 1], ring[at]) for at in range(out_size)]
    pieces_out = cut(own, spans) if chips > 1 else []

    slots = [activations]
    if line:
        slots.append(lax.ppermute(activations, "out", turn))
    else:
        slots = [lax.all_gather(activations, "out", axis=1, tiled=True)]

    def step_along(mark):
        if not line or len(slots) == out_size:
            return []
        slots[-1] = ended = after(slots[-1], mark)
        slots.append(lax.ppermute(ended, "out", turn))
        return [ended]

    coming = []
    if chips > 1:
        coming = [[shift(piece, by) for by in range(1, chips)] for piece in pieces_out]
    waiting = []

    def receive(mark, count=1):
        ended = []
        for _ in range(min(count, len(coming))):
            pieces = [halve(piece, mark, *waiting) for piece in coming.pop(0)]
            for halves in zip(*pieces):
                for half in halves:
                    waiting.extend([half, flip(half)] if pair == 2 else [half])
            ended += [halves[0] for halves in pieces]
        return ended

    room = max(depth, STRIP_ROWS if depth >= STRIP_ROWS // 2 else 0)
    plans = [plan_of(query, 1, 0, depth, width, depth) for query in range(queries)]
    chosen = []
    for count in GROUPS + (1,) * chunks:
        group, spans = (spans[:count], spans[count:]) if chips > 1 else ([], [])
        if group:
            chosen.append(count)
            length = sum(length for _, length in group)
            plans.append(plan_of(0, queries, group[0][0], length, width, room))
    plans.append(None)

    slot, laid = load(pieces_out or [own], pair * rows, query_grads, plans[0], room)
    sums = []
    mark = None
    for query in range(queries):
        others = []
        if query > 0:
            others = receive(mark) + step_along(mark)
        near_sum, mark, slot, laid = project(
            near if query == 0 else [], pair * rows, query_grads, plans[query], plans[query + 1], slot, None, others, laid
        )
        sums.append(near_sum)
    running = None
    got = min(queries - 1, len(coming))
    for at, count in enumerate(chosen):
        others = receive(mark, count - (got if at == 0 else 0)) + (step_along(mark) if at > 0 else [])
        running, mark, slot = project(
            waiting, (inp_size - pair) * rows, query_grads, plans[queries + at], plans[queries + at + 1], slot, running, others
        )
        waiting.clear()
    if running is not None:
        sums.append(running)
    raw = score(sums, slots, ring, inp_size, pair, queries, blocks, shard)
    raw = raw.reshape(inp_size, queries, blocks, shard).transpose(1, 2, 0, 3).reshape(queries, blocks, tokens)
    raw = xor_sum(xor_sum(raw, "inp", inp_size), "out", out_size)
    equal = token_ids[:, :, None] == token_ids[:, None, :]
    counts = jnp.sum(equal.astype(jnp.int32), axis=2)
    weight = loss_mask.astype(jnp.float32) / counts.astype(jnp.float32)
    return raw * weight[None]


def solution(mesh):
    in_specs = (
        P("grp", "out", "inp"),
        P("grp", "inp", "out"),
        P(None, "out", "inp"),
        P("grp", None),
        P("grp", None),
    )
    out_specs = P(None, "grp", None)
    body = functools.partial(shards, mesh.shape["inp"], mesh.shape["out"])
    return jax.shard_map(body, mesh=mesh, in_specs=in_specs, out_specs=out_specs, check_vma=False)
```

```python
import functools
import typing

import jax
import jax.numpy as jnp
from jax import lax
from jax.experimental import pallas as pl
from jax.experimental.pallas import tpu as pltpu
from jax.sharding import PartitionSpec as P

WEIGHTS = (8, 7, 8, 5)
GROUPS = (2, 1, 1)
HELPER_VMEM = 1024 * 1024
TILE = 512
STRIP_ROWS = 8192


def tile_of(length, most):
    size = min(length, most)
    while length % size:
        size -= 128
    return size


class Plan(typing.NamedTuple):
    query: int
    queries: int
    begin: int
    depth: int
    tile: int
    strips: int
    turns: int

    @property
    def steps(self):
        return self.queries * self.turns


def plan_of(query, queries, begin, depth, width, room):
    tile = tile_of(width, TILE)
    strips = 1
    while strips * 2 * depth <= room and width // tile % (strips * 2) == 0:
        strips *= 2
    return Plan(query, queries, begin, depth, tile, strips, width // tile // strips)


def fetches(plan, step, q_ref, slot_ref, sems):
    number, turn = plan.query + step // plan.turns, step % plan.turns
    copies = []
    for strip in range(plan.strips):
        column = (turn * plan.strips + strip) * plan.tile
        if not isinstance(column, int):
            column = pl.multiple_of(column, plan.tile)
        source = q_ref.at[number, pl.ds(plan.begin, plan.depth), pl.ds(column, plan.tile)]
        target = slot_ref.at[pl.ds(strip * plan.depth, plan.depth)]
        copies.append(pltpu.make_async_copy(source, target, sems.at[strip]))
    return copies


def run(copies, start):
    for copy in copies:
        if start:
            copy.start()
        else:
            copy.wait()


def load_kernel(plan, parts, *refs):
    g_refs, (q_ref, slot_ref, x_ref, sems, slot_sems) = refs[:parts], refs[parts:]
    copies = fetches(plan, 0, q_ref, slot_ref, slot_sems)
    column = 0
    for at, g_ref in enumerate(g_refs):
        rows, columns = g_ref.shape
        where = x_ref.at[pl.ds(0, rows), pl.ds(column, columns)]
        copies.append(pltpu.make_async_copy(g_ref, where, sems.at[at]))
        column += columns
    run(copies, True)
    run(copies, False)


def load(own, total, query_grads, plan, room):
    vmem_spec = pl.BlockSpec(memory_space=pltpu.VMEM)
    depth = sum(part.shape[1] for part in own)
    return pl.pallas_call(
        functools.partial(load_kernel, plan, len(own)),
        in_specs=[pl.BlockSpec(memory_space=pl.ANY)] * (len(own) + 1),
        out_specs=[vmem_spec] * 2,
        out_shape=[
            jax.ShapeDtypeStruct((room, plan.tile), jnp.bfloat16),
            jax.ShapeDtypeStruct((total, depth), jnp.bfloat16),
        ],
        scratch_shapes=[pltpu.SemaphoreType.DMA((len(own),)), pltpu.SemaphoreType.DMA((plan.strips,))],
        cost_estimate=pl.CostEstimate(flops=1024, bytes_accessed=1024, transcendentals=0),
        compiler_params=pltpu.CompilerParams(vmem_limit_bytes=HELPER_VMEM),
        name="load",
    )(*own, query_grads)


def project_kernel(parts, plan, later, fresh, laid, *refs):
    g_refs, q_ref = refs[:parts], refs[parts]
    sum_ref, mark_ref, slot_a, x_ref, slot_b, sems, sems_a, sems_b = refs[-8:]
    total = x_ref.shape[0]
    copies = []
    together = total // g_refs[0].shape[0] if parts and not laid else 1
    column = 0
    for at, g_ref in enumerate(g_refs):
        rows = g_ref.shape[0]
        row = total - rows if laid else at % together * rows
        where = x_ref.at[pl.ds(row, rows), pl.ds(column, g_ref.shape[1])]
        copies.append(pltpu.make_async_copy(g_ref, where, sems.at[at]))
        if not laid and at % together == together - 1:
            column += g_ref.shape[1]
    steps = plan.steps
    run(copies, True)
    if steps > 1:
        run(fetches(plan, 1, q_ref, slot_b, sems_b), True)
    mark_ref[...] = jnp.zeros_like(mark_ref)
    run(copies, False)

    def multiply(step, slot_ref):
        number, turn = step // plan.turns, step % plan.turns
        for strip in range(plan.strips):
            product = jnp.dot(
                x_ref[...],
                slot_ref[strip * plan.depth:(strip + 1) * plan.depth, :],
                preferred_element_type=jnp.float32,
            )
            begin = (turn * plan.strips + strip) * plan.tile
            if not isinstance(begin, int):
                begin = pl.multiple_of(begin, plan.tile)
            where = (number, slice(None), pl.ds(begin, plan.tile))
            if fresh:
                sum_ref[where] = product
            else:
                sum_ref[where] += product

    def both(pair):
        step = pair * 2

        @pl.when(pair > 0)
        def _():
            run(fetches(plan, step + 1, q_ref, slot_b, sems_b), True)
            run(fetches(plan, step, q_ref, slot_a, sems_a), False)

        multiply(step, slot_a)

        @pl.when(step + 2 < steps)
        def _():
            run(fetches(plan, step + 2, q_ref, slot_a, sems_a), True)

        if later is not None:

            @pl.when(step + 2 >= steps)
            def _():
                run(fetches(later, 0, q_ref, slot_a, sems_a), True)

        run(fetches(plan, step + 1, q_ref, slot_b, sems_b), False)
        multiply(step + 1, slot_b)

    if steps % 2 == 0:

        @pl.loop(0, steps // 2)
        def _(pair):
            both(pair)
    else:
        for step in range(steps):
            slot_ref, slot_sems = (slot_a, sems_a) if step % 2 == 0 else (slot_b, sems_b)
            if step > 0:
                run(fetches(plan, step, q_ref, slot_ref, slot_sems), step > 1)
                if step > 1:
                    run(fetches(plan, step, q_ref, slot_ref, slot_sems), False)
            multiply(step, slot_ref)
        if later is not None:
            run(fetches(later, 0, q_ref, slot_a, sems_a), True)
    if later is not None:
        run(fetches(later, 0, q_ref, slot_a, sems_a), False)


def project(parts, rows, query_grads, plan, later, slot, running, others=(), laid=None):
    width = query_grads.shape[2]
    fresh = running is None
    any_spec = pl.BlockSpec(memory_space=pl.ANY)
    vmem_spec = pl.BlockSpec(memory_space=pltpu.VMEM)
    operands = [*parts, query_grads, slot]
    in_specs = [any_spec] * (len(parts) + 1) + [vmem_spec]
    aliases = {len(parts) + 1: 2}
    if not fresh:
        aliases[len(operands)] = 0
        operands.append(running)
        in_specs.append(vmem_spec)
    out_shape = [
        jax.ShapeDtypeStruct((plan.queries, rows, width), jnp.float32),
        jax.ShapeDtypeStruct((8, 128), jnp.float32),
        jax.ShapeDtypeStruct(slot.shape, slot.dtype),
    ]
    scratch = []
    if laid is not None:
        aliases[len(operands)] = 3
        operands.append(laid)
        in_specs.append(vmem_spec)
        out_shape.append(jax.ShapeDtypeStruct(laid.shape, laid.dtype))
    else:
        scratch.append(pltpu.VMEM((rows, plan.depth), jnp.bfloat16))
    scratch += [
        pltpu.VMEM(slot.shape, slot.dtype),
        pltpu.SemaphoreType.DMA((max(len(parts), 1),)),
        pltpu.SemaphoreType.DMA((max(plan.strips, later.strips if later else 1),)),
        pltpu.SemaphoreType.DMA((plan.strips,)),
    ]
    limit = 2 * slot.size + (2 * rows * plan.depth if laid is None else 0) + 4 * 1024 * 1024
    return pl.pallas_call(
        functools.partial(project_kernel, len(parts), plan, later, fresh, laid is not None),
        in_specs=in_specs + [any_spec] * len(others),
        out_specs=[vmem_spec] * len(out_shape),
        out_shape=out_shape,
        scratch_shapes=scratch,
        input_output_aliases=aliases,
        cost_estimate=pl.CostEstimate(flops=1024, bytes_accessed=1024, transcendentals=0),
        compiler_params=pltpu.CompilerParams(vmem_limit_bytes=limit),
        name="project",
    )(*operands, *others)


def score_kernel(inp_size, pair, queries, ring, *refs):
    near_refs, refs = refs[:queries], refs[queries:]
    if inp_size > pair:
        far_ref, refs = refs[0], refs[1:]
    *a_refs, out_ref, held, sems = refs
    blocks, shard, width = held.shape[1:]
    me, here = lax.axis_index("inp"), lax.axis_index("out")
    sources = []
    for number in range(inp_size):
        by, other = divmod(number, pair)
        source = lax.rem(me - pair * by + inp_size, inp_size)
        sources.append(jnp.bitwise_xor(source, other) if pair == 2 else source)

    def bring(number):
        source = sources[number]
        if len(a_refs) == 1:
            begin = pl.multiple_of(source * shard, shard)
            pltpu.make_async_copy(
                a_refs[0].at[:, pl.ds(begin, shard), :], held.at[number], sems.at[number]
            ).start()
            return
        for at, a_ref in enumerate(a_refs):
            for place, spot in enumerate(ring):

                @pl.when((here == spot) & (source == ring[place - at]))
                def _(a_ref=a_ref):
                    pltpu.make_async_copy(a_ref, held.at[number], sems.at[number]).start()

    lanes = 128
    bring(0)
    for number, source in enumerate(sources):
        if number + 1 < inp_size:
            bring(number + 1)
        pltpu.make_async_copy(held.at[number], held.at[number], sems.at[number]).wait()
        totals = [None] * queries
        begin = (number if number < pair else number - pair) * blocks * shard
        for at in range(0, width, lanes):
            block = held[number, :, :, at:at + lanes].reshape(blocks * shard, lanes).astype(jnp.float32)
            for query in range(queries):
                where = (slice(begin, begin + blocks * shard), slice(at, at + lanes))
                rows = near_refs[query][(0, *where)] if number < pair else far_ref[(query, *where)]
                term = rows * block
                totals[query] = term if totals[query] is None else totals[query] + term
        for query in range(queries):
            out_ref[source, query, :] = jnp.sum(totals[query].T, axis=0)


def score(sums, slots, ring, inp_size, pair, queries, blocks, shard):
    width = sums[0].shape[2]
    return pl.pallas_call(
        functools.partial(score_kernel, inp_size, pair, queries, ring),
        in_specs=[pl.BlockSpec(memory_space=pltpu.VMEM)] * len(sums)
        + [pl.BlockSpec(memory_space=pl.ANY)] * len(slots),
        out_specs=pl.BlockSpec(memory_space=pltpu.VMEM),
        out_shape=jax.ShapeDtypeStruct((inp_size, queries, blocks * shard), jnp.float32),
        scratch_shapes=[
            pltpu.VMEM((inp_size, blocks, shard, width), jnp.bfloat16),
            pltpu.SemaphoreType.DMA((inp_size,)),
        ],
        compiler_params=pltpu.CompilerParams(vmem_limit_bytes=6 * 1024 * 1024),
        name="score",
    )(*sums, *slots)


def xor_sum(value, axis, size):
    if size & (size - 1):
        return lax.psum(value, axis)
    terms = [value]
    for other in range(1, size):
        terms.append(lax.ppermute(value, axis, [(at, at ^ other) for at in range(size)]))
    while len(terms) > 1:
        terms = [terms[at] + terms[at + 1] for at in range(0, len(terms), 2)]
    return terms[0]


def after(value, *others):
    any_spec = pl.BlockSpec(memory_space=pl.ANY)
    return pl.pallas_call(
        lambda *refs: None,
        in_specs=[any_spec] * (1 + len(others)),
        out_specs=any_spec,
        out_shape=jax.ShapeDtypeStruct(value.shape, value.dtype),
        input_output_aliases={0: 0},
        compiler_params=pltpu.CompilerParams(vmem_limit_bytes=HELPER_VMEM),
        name="after",
    )(pltpu.with_memory_space_constraint(value, pltpu.VMEM), *others)


def halve_kernel(source_ref, *refs):
    *outs, sems = refs[-3:]
    begin, copies = 0, []
    for at, out_ref in enumerate(outs):
        where = source_ref.at[:, pl.ds(begin, out_ref.shape[1])]
        copies.append(pltpu.make_async_copy(where, out_ref, sems.at[at]))
        begin += out_ref.shape[1]
    run(copies, True)
    run(copies, False)


def halve(value, *others):
    rows, columns = value.shape
    first = columns // 256 * 128 or columns
    if first == columns:
        return [after(value, *others)]
    return pl.pallas_call(
        halve_kernel,
        in_specs=[pl.BlockSpec(memory_space=pl.ANY)] * (1 + len(others)),
        out_specs=[pl.BlockSpec(memory_space=pltpu.VMEM)] * 2,
        out_shape=[jax.ShapeDtypeStruct((rows, part), value.dtype) for part in (first, columns - first)],
        scratch_shapes=[pltpu.SemaphoreType.DMA((2,))],
        cost_estimate=pl.CostEstimate(flops=1024, bytes_accessed=1024, transcendentals=0),
        compiler_params=pltpu.CompilerParams(vmem_limit_bytes=HELPER_VMEM),
        name="halve",
    )(pltpu.with_memory_space_constraint(value, pltpu.VMEM), *others)


def in_hbm(value):
    return pltpu.with_memory_space_constraint(value, pltpu.HBM)


def cut_kernel(spans, source_ref, *refs):
    outs, sems = refs[:-1], refs[-1]
    copies = []
    for at, (span, out_ref) in enumerate(zip(spans, outs)):
        copies.append(pltpu.make_async_copy(source_ref.at[:, pl.ds(*span)], out_ref, sems.at[at]))
    run(copies, True)
    run(copies, False)


def cut(source, spans):
    return pl.pallas_call(
        functools.partial(cut_kernel, spans),
        in_specs=[pl.BlockSpec(memory_space=pl.ANY)],
        out_specs=[pl.BlockSpec(memory_space=pltpu.VMEM)] * len(spans),
        out_shape=[jax.ShapeDtypeStruct((source.shape[0], length), source.dtype) for _, length in spans],
        scratch_shapes=[pltpu.SemaphoreType.DMA((len(spans),))],
        compiler_params=pltpu.CompilerParams(vmem_limit_bytes=HELPER_VMEM),
        name="cut",
    )(source)


def shards(inp_size, out_size, activations, out_grads, query_grads, token_ids, loss_mask):
    blocks, shard, depth = out_grads.shape
    queries, _, width = query_grads.shape
    tokens = token_ids.shape[1]
    pair = 2 if inp_size % 2 == 0 else 1
    chips = inp_size // pair
    rows = blocks * shard

    unit = 256 if depth % 256 == 0 else depth
    units = depth // unit
    edges = [0]
    for at in range(len(WEIGHTS)):
        edges.append(units * sum(WEIGHTS[:at + 1]) // sum(WEIGHTS) * unit)
    spans = [(begin, end - begin) for begin, end in zip(edges, edges[1:]) if end > begin]
    chunks = len(spans)

    def flip(value):
        return lax.ppermute(value, "inp", [(at, at ^ 1) for at in range(inp_size)])

    def shift(value, by):
        return lax.ppermute(value, "inp", [(at, (at + pair * by) % inp_size) for at in range(inp_size)])

    own = in_hbm(out_grads.reshape(rows, depth))
    near = [pltpu.with_memory_space_constraint(flip(own), pltpu.VMEM)] if pair == 2 else []
    query_grads = in_hbm(query_grads)
    activations = in_hbm(activations)
    line = inp_size == out_size and activations.shape[1] == shard and out_size > 1
    ring = list(range(0, out_size, 2)) + list(range(1, out_size, 2))[::-1]
    turn = [(ring[at - 1], ring[at]) for at in range(out_size)]
    pieces_out = []
    if chips > 1:
        pieces_out = cut(own, spans[:1]) + (cut(own, spans[1:]) if chunks > 1 else [])

    slots = [activations]
    if line:
        slots.append(lax.ppermute(activations, "out", turn))
    else:
        slots = [lax.all_gather(activations, "out", axis=1, tiled=True)]

    def step_along(mark):
        if not line or len(slots) == out_size:
            return []
        slots[-1] = ended = after(slots[-1], mark)
        slots.append(lax.ppermute(ended, "out", turn))
        return [ended]

    coming = []
    if chips > 1:
        coming = [[shift(piece, by) for by in range(1, chips)] for piece in pieces_out]
    waiting = []

    def receive(mark, count=1):
        ended = []
        for _ in range(min(count, len(coming))):
            pieces = [halve(piece, mark, *waiting) for piece in coming.pop(0)]
            for halves in zip(*pieces):
                for half in halves:
                    waiting.extend([half, flip(half)] if pair == 2 else [half])
            ended += [halves[0] for halves in pieces]
        return ended

    room = max(depth, STRIP_ROWS if depth >= STRIP_ROWS // 2 else 0)
    plans = [plan_of(query, 1, 0, depth, width, depth) for query in range(queries)]
    chosen = []
    for count in GROUPS + (1,) * chunks:
        group, spans = (spans[:count], spans[count:]) if chips > 1 else ([], [])
        if group:
            chosen.append(count)
            length = sum(length for _, length in group)
            plans.append(plan_of(0, queries, group[0][0], length, width, room))
    plans.append(None)

    slot, laid = load(pieces_out or [own], pair * rows, query_grads, plans[0], room)
    sums = []
    mark = None
    for query in range(queries):
        others = []
        if query > 0:
            others = receive(mark) + step_along(mark)
        near_sum, mark, slot, laid = project(
            near if query == 0 else [], pair * rows, query_grads, plans[query], plans[query + 1], slot, None, others, laid
        )
        sums.append(near_sum)
    running = None
    got = min(queries - 1, len(coming))
    for at, count in enumerate(chosen):
        others = receive(mark, count - (got if at == 0 else 0)) + (step_along(mark) if at > 0 else [])
        running, mark, slot = project(
            waiting, (inp_size - pair) * rows, query_grads, plans[queries + at], plans[queries + at + 1], slot, running, others
        )
        waiting.clear()
    if running is not None:
        sums.append(running)
    raw = score(sums, slots, ring, inp_size, pair, queries, blocks, shard)
    raw = raw.reshape(inp_size, queries, blocks, shard).transpose(1, 2, 0, 3).reshape(queries, blocks, tokens)
    raw = xor_sum(xor_sum(raw, "inp", inp_size), "out", out_size)
    equal = token_ids[:, :, None] == token_ids[:, None, :]
    counts = jnp.sum(equal.astype(jnp.int32), axis=2)
    weight = loss_mask.astype(jnp.float32) / counts.astype(jnp.float32)
    return raw * weight[None]


def solution(mesh):
    in_specs = (
        P("grp", "out", "inp"),
        P("grp", "inp", "out"),
        P(None, "out", "inp"),
        P("grp", None),
        P("grp", None),
    )
    out_specs = P(None, "grp", None)
    body = functools.partial(shards, mesh.shape["inp"], mesh.shape["out"])
    return jax.shard_map(body, mesh=mesh, in_specs=in_specs, out_specs=out_specs, check_vma=False)
```

```python
import functools
import typing

import jax
import jax.numpy as jnp
from jax import lax
from jax.experimental import pallas as pl
from jax.experimental.pallas import tpu as pltpu
from jax.sharding import PartitionSpec as P

WEIGHTS = (9, 6, 7, 6)
GROUPS = (2, 1, 1)
HELPER_VMEM = 1024 * 1024
TILE = 512
STRIP_ROWS = 8192


def tile_of(length, most):
    size = min(length, most)
    while length % size:
        size -= 128
    return size


class Plan(typing.NamedTuple):
    first: int
    steps: int
    begin: int
    depth: int
    tile: int
    strips: int
    turns: int


def plan_of(queries, begin, depth, width, room):
    tile = tile_of(width, TILE)
    strips = 1
    while strips * 2 * depth <= room and width // tile % (strips * 2) == 0:
        strips *= 2
    turns = width // tile // strips
    return Plan(0, queries * turns, begin, depth, tile, strips, turns)


def fetches(plan, step, q_ref, slot_ref, sems):
    number, turn = (plan.first + step) // plan.turns, (plan.first + step) % plan.turns
    copies = []
    for strip in range(plan.strips):
        column = (turn * plan.strips + strip) * plan.tile
        if not isinstance(column, int):
            column = pl.multiple_of(column, plan.tile)
        source = q_ref.at[number, pl.ds(plan.begin, plan.depth), pl.ds(column, plan.tile)]
        target = slot_ref.at[pl.ds(strip * plan.depth, plan.depth)]
        copies.append(pltpu.make_async_copy(source, target, sems.at[strip]))
    return copies


def run(copies, start):
    for copy in copies:
        if start:
            copy.start()
        else:
            copy.wait()


def load_kernel(plan, parts, *refs):
    g_refs, (q_ref, slot_ref, x_ref, sems, slot_sems) = refs[:parts], refs[parts:]
    copies = fetches(plan, 0, q_ref, slot_ref, slot_sems)
    column = 0
    for at, g_ref in enumerate(g_refs):
        rows, columns = g_ref.shape
        where = x_ref.at[pl.ds(0, rows), pl.ds(column, columns)]
        copies.append(pltpu.make_async_copy(g_ref, where, sems.at[at]))
        column += columns
    run(copies, True)
    run(copies, False)


def load(own, total, query_grads, plan, room):
    vmem_spec = pl.BlockSpec(memory_space=pltpu.VMEM)
    depth = sum(part.shape[1] for part in own)
    return pl.pallas_call(
        functools.partial(load_kernel, plan, len(own)),
        in_specs=[pl.BlockSpec(memory_space=pl.ANY)] * (len(own) + 1),
        out_specs=[vmem_spec] * 2,
        out_shape=[
            jax.ShapeDtypeStruct((room, plan.tile), jnp.bfloat16),
            jax.ShapeDtypeStruct((total, depth), jnp.bfloat16),
        ],
        scratch_shapes=[pltpu.SemaphoreType.DMA((len(own),)), pltpu.SemaphoreType.DMA((plan.strips,))],
        cost_estimate=pl.CostEstimate(flops=1024, bytes_accessed=1024, transcendentals=0),
        compiler_params=pltpu.CompilerParams(vmem_limit_bytes=HELPER_VMEM),
        name="load",
    )(*own, query_grads)


def project_kernel(parts, plan, later, add, laid, *refs):
    g_refs, q_ref = refs[:parts], refs[parts]
    sum_ref, mark_ref, slot_a, x_ref, slot_b, sems, sems_a, sems_b = refs[-8:]
    total = x_ref.shape[0]
    copies = []
    together = total // g_refs[0].shape[0] if parts and not laid else 1
    column = 0
    for at, g_ref in enumerate(g_refs):
        rows = g_ref.shape[0]
        row = total - rows if laid else at % together * rows
        where = x_ref.at[pl.ds(row, rows), pl.ds(column, g_ref.shape[1])]
        copies.append(pltpu.make_async_copy(g_ref, where, sems.at[at]))
        if not laid and at % together == together - 1:
            column += g_ref.shape[1]
    steps = plan.steps
    run(copies, True)
    if steps > 1:
        run(fetches(plan, 1, q_ref, slot_b, sems_b), True)
    mark_ref[...] = jnp.zeros_like(mark_ref)
    run(copies, False)

    def multiply(step, slot_ref):
        number, turn = (plan.first + step) // plan.turns, (plan.first + step) % plan.turns
        for strip in range(plan.strips):
            product = jnp.dot(
                x_ref[...],
                slot_ref[strip * plan.depth:(strip + 1) * plan.depth, :],
                preferred_element_type=jnp.float32,
            )
            begin = (turn * plan.strips + strip) * plan.tile
            if not isinstance(begin, int):
                begin = pl.multiple_of(begin, plan.tile)
            where = (number, slice(None), pl.ds(begin, plan.tile))
            if add:
                sum_ref[where] += product
            else:
                sum_ref[where] = product

    def both(pair):
        step = pair * 2

        @pl.when(pair > 0)
        def _():
            run(fetches(plan, step + 1, q_ref, slot_b, sems_b), True)
            run(fetches(plan, step, q_ref, slot_a, sems_a), False)

        multiply(step, slot_a)

        @pl.when(step + 2 < steps)
        def _():
            run(fetches(plan, step + 2, q_ref, slot_a, sems_a), True)

        if later is not None:

            @pl.when(step + 2 >= steps)
            def _():
                run(fetches(later, 0, q_ref, slot_a, sems_a), True)

        run(fetches(plan, step + 1, q_ref, slot_b, sems_b), False)
        multiply(step + 1, slot_b)

    if steps % 2 == 0:

        @pl.loop(0, steps // 2)
        def _(pair):
            both(pair)
    else:
        for step in range(steps):
            slot_ref, slot_sems = (slot_a, sems_a) if step % 2 == 0 else (slot_b, sems_b)
            if step > 0:
                run(fetches(plan, step, q_ref, slot_ref, slot_sems), step > 1)
                if step > 1:
                    run(fetches(plan, step, q_ref, slot_ref, slot_sems), False)
            multiply(step, slot_ref)
        if later is not None:
            run(fetches(later, 0, q_ref, slot_a, sems_a), True)
    if later is not None:
        run(fetches(later, 0, q_ref, slot_a, sems_a), False)


def project(parts, rows, query_grads, plan, later, slot, running, others=(), laid=None):
    queries, _, width = query_grads.shape
    fresh = running is None
    any_spec = pl.BlockSpec(memory_space=pl.ANY)
    vmem_spec = pl.BlockSpec(memory_space=pltpu.VMEM)
    operands = [*parts, query_grads, slot]
    in_specs = [any_spec] * (len(parts) + 1) + [vmem_spec]
    aliases = {len(parts) + 1: 2}
    if not fresh:
        aliases[len(operands)] = 0
        operands.append(running)
        in_specs.append(vmem_spec)
    out_shape = [
        jax.ShapeDtypeStruct((queries, rows, width), jnp.float32),
        jax.ShapeDtypeStruct((8, 128), jnp.float32),
        jax.ShapeDtypeStruct(slot.shape, slot.dtype),
    ]
    scratch = []
    if laid is not None:
        aliases[len(operands)] = 3
        operands.append(laid)
        in_specs.append(vmem_spec)
        out_shape.append(jax.ShapeDtypeStruct(laid.shape, laid.dtype))
    else:
        scratch.append(pltpu.VMEM((rows, plan.depth), jnp.bfloat16))
    scratch += [
        pltpu.VMEM(slot.shape, slot.dtype),
        pltpu.SemaphoreType.DMA((max(len(parts), 1),)),
        pltpu.SemaphoreType.DMA((max(plan.strips, later.strips if later else 1),)),
        pltpu.SemaphoreType.DMA((plan.strips,)),
    ]
    limit = 2 * slot.size + (2 * rows * plan.depth if laid is None else 0) + 4 * 1024 * 1024
    return pl.pallas_call(
        functools.partial(
            project_kernel, len(parts), plan, later, not fresh and laid is None, laid is not None
        ),
        in_specs=in_specs + [any_spec] * len(others),
        out_specs=[vmem_spec] * len(out_shape),
        out_shape=out_shape,
        scratch_shapes=scratch,
        input_output_aliases=aliases,
        cost_estimate=pl.CostEstimate(flops=1024, bytes_accessed=1024, transcendentals=0),
        compiler_params=pltpu.CompilerParams(vmem_limit_bytes=limit),
        name="project",
    )(*operands, *others)


def score_kernel(inp_size, pair, queries, ring, *refs):
    near_ref, refs = refs[0], refs[1:]
    if inp_size > pair:
        far_ref, refs = refs[0], refs[1:]
    *a_refs, out_ref, held, sems = refs
    blocks, shard, width = held.shape[1:]
    me, here = lax.axis_index("inp"), lax.axis_index("out")
    sources = []
    for number in range(inp_size):
        by, other = divmod(number, pair)
        source = lax.rem(me - pair * by + inp_size, inp_size)
        sources.append(jnp.bitwise_xor(source, other) if pair == 2 else source)

    def bring(number):
        source = sources[number]
        if len(a_refs) == 1:
            begin = pl.multiple_of(source * shard, shard)
            pltpu.make_async_copy(
                a_refs[0].at[:, pl.ds(begin, shard), :], held.at[number], sems.at[number]
            ).start()
            return
        for at, a_ref in enumerate(a_refs):
            for place, spot in enumerate(ring):

                @pl.when((here == spot) & (source == ring[place - at]))
                def _(a_ref=a_ref):
                    pltpu.make_async_copy(a_ref, held.at[number], sems.at[number]).start()

    lanes = 128
    bring(0)
    for number, source in enumerate(sources):
        if number + 1 < inp_size:
            bring(number + 1)
        pltpu.make_async_copy(held.at[number], held.at[number], sems.at[number]).wait()
        totals = [None] * queries
        begin = (number if number < pair else number - pair) * blocks * shard
        for at in range(0, width, lanes):
            block = held[number, :, :, at:at + lanes].reshape(blocks * shard, lanes).astype(jnp.float32)
            for query in range(queries):
                where = (slice(begin, begin + blocks * shard), slice(at, at + lanes))
                rows = (near_ref if number < pair else far_ref)[(query, *where)]
                term = rows * block
                totals[query] = term if totals[query] is None else totals[query] + term
        for query in range(queries):
            out_ref[source, query, :] = jnp.sum(totals[query].T, axis=0)


def score(sums, slots, ring, inp_size, pair, queries, blocks, shard):
    width = sums[0].shape[2]
    return pl.pallas_call(
        functools.partial(score_kernel, inp_size, pair, queries, ring),
        in_specs=[pl.BlockSpec(memory_space=pltpu.VMEM)] * len(sums)
        + [pl.BlockSpec(memory_space=pl.ANY)] * len(slots),
        out_specs=pl.BlockSpec(memory_space=pltpu.VMEM),
        out_shape=jax.ShapeDtypeStruct((inp_size, queries, blocks * shard), jnp.float32),
        scratch_shapes=[
            pltpu.VMEM((inp_size, blocks, shard, width), jnp.bfloat16),
            pltpu.SemaphoreType.DMA((inp_size,)),
        ],
        compiler_params=pltpu.CompilerParams(vmem_limit_bytes=6 * 1024 * 1024),
        name="score",
    )(*sums, *slots)


def xor_sum(value, axis, size):
    if size & (size - 1):
        return lax.psum(value, axis)
    terms = [value]
    for other in range(1, size):
        terms.append(lax.ppermute(value, axis, [(at, at ^ other) for at in range(size)]))
    while len(terms) > 1:
        terms = [terms[at] + terms[at + 1] for at in range(0, len(terms), 2)]
    return terms[0]


def after(value, *others):
    any_spec = pl.BlockSpec(memory_space=pl.ANY)
    return pl.pallas_call(
        lambda *refs: None,
        in_specs=[any_spec] * (1 + len(others)),
        out_specs=any_spec,
        out_shape=jax.ShapeDtypeStruct(value.shape, value.dtype),
        input_output_aliases={0: 0},
        compiler_params=pltpu.CompilerParams(vmem_limit_bytes=HELPER_VMEM),
        name="after",
    )(pltpu.with_memory_space_constraint(value, pltpu.VMEM), *others)


def halve_kernel(source_ref, *refs):
    *outs, sems = refs[-3:]
    begin, copies = 0, []
    for at, out_ref in enumerate(outs):
        where = source_ref.at[:, pl.ds(begin, out_ref.shape[1])]
        copies.append(pltpu.make_async_copy(where, out_ref, sems.at[at]))
        begin += out_ref.shape[1]
    run(copies, True)
    run(copies, False)


def halve(value, *others):
    rows, columns = value.shape
    first = columns // 256 * 128 or columns
    if first == columns:
        return [after(value, *others)]
    return pl.pallas_call(
        halve_kernel,
        in_specs=[pl.BlockSpec(memory_space=pl.ANY)] * (1 + len(others)),
        out_specs=[pl.BlockSpec(memory_space=pltpu.VMEM)] * 2,
        out_shape=[jax.ShapeDtypeStruct((rows, part), value.dtype) for part in (first, columns - first)],
        scratch_shapes=[pltpu.SemaphoreType.DMA((2,))],
        cost_estimate=pl.CostEstimate(flops=1024, bytes_accessed=1024, transcendentals=0),
        compiler_params=pltpu.CompilerParams(vmem_limit_bytes=HELPER_VMEM),
        name="halve",
    )(pltpu.with_memory_space_constraint(value, pltpu.VMEM), *others)


def in_hbm(value):
    return pltpu.with_memory_space_constraint(value, pltpu.HBM)


def cut_kernel(spans, total, source_ref, a_ref, *refs):
    outs, sems = refs[-1 - total:-1], refs[-1]
    copies = []
    for at, out_ref in enumerate(outs):
        piece = source_ref.at[:, pl.ds(*spans[at])] if at < len(spans) else a_ref
        copies.append(pltpu.make_async_copy(piece, out_ref, sems.at[at]))
    run(copies, True)
    run(copies, False)


def cut(source, spans, activations, copied, *others):
    shapes = [(source.shape[0], length) for _, length in spans] + [activations.shape] * copied
    return pl.pallas_call(
        functools.partial(cut_kernel, spans, len(shapes)),
        in_specs=[pl.BlockSpec(memory_space=pl.ANY)] * (2 + len(others)),
        out_specs=[pl.BlockSpec(memory_space=pltpu.VMEM)] * len(shapes),
        out_shape=[jax.ShapeDtypeStruct(shape, source.dtype) for shape in shapes],
        scratch_shapes=[pltpu.SemaphoreType.DMA((len(shapes),))],
        compiler_params=pltpu.CompilerParams(vmem_limit_bytes=HELPER_VMEM),
        name="cut",
    )(source, activations, *others)


def shards(inp_size, out_size, activations, out_grads, query_grads, token_ids, loss_mask):
    blocks, shard, depth = out_grads.shape
    queries, _, width = query_grads.shape
    tokens = token_ids.shape[1]
    pair = 2 if inp_size % 2 == 0 else 1
    chips = inp_size // pair
    rows = blocks * shard

    unit = 256 if depth % 256 == 0 else depth
    units = depth // unit
    edges = [0]
    for at in range(len(WEIGHTS)):
        edges.append(units * sum(WEIGHTS[:at + 1]) // sum(WEIGHTS) * unit)
    spans = [(begin, end - begin) for begin, end in zip(edges, edges[1:]) if end > begin]
    chunks = len(spans)

    def flip(value):
        return lax.ppermute(value, "inp", [(at, at ^ 1) for at in range(inp_size)])

    def shift(value, by):
        return lax.ppermute(value, "inp", [(at, (at + pair * by) % inp_size) for at in range(inp_size)])

    own = in_hbm(out_grads.reshape(rows, depth))
    near = [pltpu.with_memory_space_constraint(flip(own), pltpu.VMEM)] if pair == 2 else []
    query_grads = in_hbm(query_grads)
    activations = in_hbm(activations)
    line = inp_size == out_size and activations.shape[1] == shard and out_size > 1
    ring = list(range(0, out_size, 2)) + list(range(1, out_size, 2))[::-1]
    turn = [(ring[at - 1], ring[at]) for at in range(out_size)]
    pieces_out = list(cut(own, spans[:1], activations, False)) if chips > 1 else []
    *rest, moving = cut(own, spans[1:] if chips > 1 else [], activations, True, *pieces_out)
    pieces_out += rest

    slots = [moving]
    if line:
        slots.append(lax.ppermute(moving, "out", turn))
    else:
        slots = [lax.all_gather(activations, "out", axis=1, tiled=True)]

    def step_along(mark):
        if not line or len(slots) == out_size:
            return []
        slots[-1] = ended = after(slots[-1], mark)
        slots.append(lax.ppermute(ended, "out", turn))
        return [ended]

    coming = []
    if chips > 1:
        coming = [[shift(piece, by) for by in range(1, chips)] for piece in pieces_out]
    waiting = []

    def receive(mark, count=1):
        ended = []
        for _ in range(min(count, len(coming))):
            pieces = [halve(piece, mark, *waiting) for piece in coming.pop(0)]
            for halves in zip(*pieces):
                for half in halves:
                    waiting.extend([half, flip(half)] if pair == 2 else [half])
            ended += [halves[0] for halves in pieces]
        return ended

    room = max(depth, STRIP_ROWS if depth >= STRIP_ROWS // 2 else 0)
    near_plan = plan_of(queries, 0, depth, width, depth)
    early = near_plan.steps * 3 // 8 * 2 or near_plan.steps
    plans = [near_plan._replace(steps=early)]
    if early < near_plan.steps:
        plans.append(near_plan._replace(first=early, steps=near_plan.steps - early))
    near_calls = len(plans)
    chosen = []
    for count in GROUPS + (1,) * chunks:
        group, spans = (spans[:count], spans[count:]) if chips > 1 else ([], [])
        if group:
            chosen.append(count)
            length = sum(length for _, length in group)
            plans.append(plan_of(queries, group[0][0], length, width, room))
    plans.append(None)

    slot, laid = load(pieces_out or [own], pair * rows, query_grads, plans[0], room)
    near_sum = None
    got = 0
    for at in range(near_calls):
        others = []
        if at > 0:
            got = min(1, len(coming))
            others = receive(mark) + step_along(mark)
        near_sum, mark, slot, laid = project(
            [] if at else near, pair * rows, query_grads, plans[at], plans[at + 1], slot, near_sum, others, laid
        )
    sums = [near_sum]
    running = None
    for at, count in enumerate(chosen):
        others = receive(mark, count - (got if at == 0 else 0)) + (step_along(mark) if at > 0 else [])
        running, mark, slot = project(
            waiting, (inp_size - pair) * rows, query_grads, plans[near_calls + at], plans[near_calls + at + 1], slot, running, others
        )
        waiting.clear()
    if running is not None:
        sums.append(running)
    raw = score(sums, slots, ring, inp_size, pair, queries, blocks, shard)
    raw = raw.reshape(inp_size, queries, blocks, shard).transpose(1, 2, 0, 3).reshape(queries, blocks, tokens)
    raw = xor_sum(xor_sum(raw, "inp", inp_size), "out", out_size)
    equal = token_ids[:, :, None] == token_ids[:, None, :]
    counts = jnp.sum(equal.astype(jnp.int32), axis=2)
    weight = loss_mask.astype(jnp.float32) / counts.astype(jnp.float32)
    return raw * weight[None]


def solution(mesh):
    in_specs = (
        P("grp", "out", "inp"),
        P("grp", "inp", "out"),
        P(None, "out", "inp"),
        P("grp", None),
        P("grp", None),
    )
    out_specs = P(None, "grp", None)
    body = functools.partial(shards, mesh.shape["inp"], mesh.shape["out"])
    return jax.shard_map(body, mesh=mesh, in_specs=in_specs, out_specs=out_specs, check_vma=False)
```

```python
import functools
import typing

import jax
import jax.numpy as jnp
from jax import lax
from jax.experimental import pallas as pl
from jax.experimental.pallas import tpu as pltpu
from jax.sharding import PartitionSpec as P

WEIGHTS = (9, 6, 7, 6)
HELPER_VMEM = 1024 * 1024
TILE = 512


def tile_of(length, most):
    size = min(length, most)
    while length % size:
        size -= 128
    return size


class Plan(typing.NamedTuple):
    first: int
    steps: int
    begin: int
    depth: int
    tile: int
    strips: int
    turns: int


def plan_of(queries, begin, depth, width, room):
    tile = tile_of(width, TILE)
    strips = 1
    while strips * 2 * depth <= room and width // tile % (strips * 2) == 0:
        strips *= 2
    turns = width // tile // strips
    return Plan(0, queries * turns, begin, depth, tile, strips, turns)


def fetches(plan, step, q_ref, slot_ref, sems):
    number, turn = (plan.first + step) // plan.turns, (plan.first + step) % plan.turns
    copies = []
    for strip in range(plan.strips):
        column = (turn * plan.strips + strip) * plan.tile
        if not isinstance(column, int):
            column = pl.multiple_of(column, plan.tile)
        source = q_ref.at[number, pl.ds(plan.begin, plan.depth), pl.ds(column, plan.tile)]
        target = slot_ref.at[pl.ds(strip * plan.depth, plan.depth)]
        copies.append(pltpu.make_async_copy(source, target, sems.at[strip]))
    return copies


def run(copies, start):
    for copy in copies:
        if start:
            copy.start()
        else:
            copy.wait()


def load_kernel(plan, parts, *refs):
    g_refs, (q_ref, slot_ref, x_ref, sems, slot_sems) = refs[:parts], refs[parts:]
    copies = fetches(plan, 0, q_ref, slot_ref, slot_sems)
    column = 0
    for at, g_ref in enumerate(g_refs):
        rows, columns = g_ref.shape
        where = x_ref.at[pl.ds(0, rows), pl.ds(column, columns)]
        copies.append(pltpu.make_async_copy(g_ref, where, sems.at[at]))
        column += columns
    run(copies, True)
    run(copies, False)


def load(own, total, query_grads, plan, room):
    vmem_spec = pl.BlockSpec(memory_space=pltpu.VMEM)
    depth = sum(part.shape[1] for part in own)
    return pl.pallas_call(
        functools.partial(load_kernel, plan, len(own)),
        in_specs=[pl.BlockSpec(memory_space=pl.ANY)] * (len(own) + 1),
        out_specs=[vmem_spec] * 2,
        out_shape=[
            jax.ShapeDtypeStruct((room, plan.tile), jnp.bfloat16),
            jax.ShapeDtypeStruct((total, depth), jnp.bfloat16),
        ],
        scratch_shapes=[pltpu.SemaphoreType.DMA((len(own),)), pltpu.SemaphoreType.DMA((plan.strips,))],
        cost_estimate=pl.CostEstimate(flops=1024, bytes_accessed=1024, transcendentals=0),
        compiler_params=pltpu.CompilerParams(vmem_limit_bytes=HELPER_VMEM),
        name="load",
    )(*own, query_grads)


def project_kernel(parts, plan, later, add, laid, *refs):
    g_refs, q_ref = refs[:parts], refs[parts]
    sum_ref, mark_ref, slot_a, x_ref, slot_b, sems, sems_a, sems_b = refs[-8:]
    total = x_ref.shape[0]
    copies = []
    together = total // g_refs[0].shape[0] if parts and not laid else 1
    column = 0
    for at, g_ref in enumerate(g_refs):
        rows = g_ref.shape[0]
        row = total - rows if laid else at % together * rows
        where = x_ref.at[pl.ds(row, rows), pl.ds(column, g_ref.shape[1])]
        copies.append(pltpu.make_async_copy(g_ref, where, sems.at[at]))
        if not laid and at % together == together - 1:
            column += g_ref.shape[1]
    steps = plan.steps
    run(copies, True)
    if steps > 1:
        run(fetches(plan, 1, q_ref, slot_b, sems_b), True)
    mark_ref[...] = jnp.zeros_like(mark_ref)
    run(copies, False)

    def multiply(step, slot_ref):
        number, turn = (plan.first + step) // plan.turns, (plan.first + step) % plan.turns
        for strip in range(plan.strips):
            product = jnp.dot(
                x_ref[...],
                slot_ref[strip * plan.depth:(strip + 1) * plan.depth, :],
                preferred_element_type=jnp.float32,
            )
            begin = (turn * plan.strips + strip) * plan.tile
            if not isinstance(begin, int):
                begin = pl.multiple_of(begin, plan.tile)
            where = (number, slice(None), pl.ds(begin, plan.tile))
            if add:
                sum_ref[where] += product
            else:
                sum_ref[where] = product

    def both(pair):
        step = pair * 2

        @pl.when(pair > 0)
        def _():
            run(fetches(plan, step + 1, q_ref, slot_b, sems_b), True)
            run(fetches(plan, step, q_ref, slot_a, sems_a), False)

        multiply(step, slot_a)

        @pl.when(step + 2 < steps)
        def _():
            run(fetches(plan, step + 2, q_ref, slot_a, sems_a), True)

        if later is not None:

            @pl.when(step + 2 >= steps)
            def _():
                run(fetches(later, 0, q_ref, slot_a, sems_a), True)

        run(fetches(plan, step + 1, q_ref, slot_b, sems_b), False)
        multiply(step + 1, slot_b)

    if steps % 2 == 0:

        @pl.loop(0, steps // 2)
        def _(pair):
            both(pair)
    else:
        for step in range(steps):
            slot_ref, slot_sems = (slot_a, sems_a) if step % 2 == 0 else (slot_b, sems_b)
            if step > 0:
                run(fetches(plan, step, q_ref, slot_ref, slot_sems), step > 1)
                if step > 1:
                    run(fetches(plan, step, q_ref, slot_ref, slot_sems), False)
            multiply(step, slot_ref)
        if later is not None:
            run(fetches(later, 0, q_ref, slot_a, sems_a), True)
    if later is not None:
        run(fetches(later, 0, q_ref, slot_a, sems_a), False)


def project(parts, rows, query_grads, plan, later, slot, running, others=(), laid=None):
    queries, _, width = query_grads.shape
    fresh = running is None
    any_spec = pl.BlockSpec(memory_space=pl.ANY)
    vmem_spec = pl.BlockSpec(memory_space=pltpu.VMEM)
    operands = [*parts, query_grads, slot]
    in_specs = [any_spec] * (len(parts) + 1) + [vmem_spec]
    aliases = {len(parts) + 1: 2}
    if not fresh:
        aliases[len(operands)] = 0
        operands.append(running)
        in_specs.append(vmem_spec)
    out_shape = [
        jax.ShapeDtypeStruct((queries, rows, width), jnp.float32),
        jax.ShapeDtypeStruct((8, 128), jnp.float32),
        jax.ShapeDtypeStruct(slot.shape, slot.dtype),
    ]
    scratch = []
    if laid is not None:
        aliases[len(operands)] = 3
        operands.append(laid)
        in_specs.append(vmem_spec)
        out_shape.append(jax.ShapeDtypeStruct(laid.shape, laid.dtype))
    else:
        scratch.append(pltpu.VMEM((rows, plan.depth), jnp.bfloat16))
    scratch += [
        pltpu.VMEM(slot.shape, slot.dtype),
        pltpu.SemaphoreType.DMA((max(len(parts), 1),)),
        pltpu.SemaphoreType.DMA((max(plan.strips, later.strips if later else 1),)),
        pltpu.SemaphoreType.DMA((plan.strips,)),
    ]
    limit = 2 * slot.size + (2 * rows * plan.depth if laid is None else 0) + 3 * 1024 * 1024
    return pl.pallas_call(
        functools.partial(
            project_kernel, len(parts), plan, later, not fresh and laid is None, laid is not None
        ),
        in_specs=in_specs + [any_spec] * len(others),
        out_specs=[vmem_spec] * len(out_shape),
        out_shape=out_shape,
        scratch_shapes=scratch,
        input_output_aliases=aliases,
        cost_estimate=pl.CostEstimate(flops=1024, bytes_accessed=1024, transcendentals=0),
        compiler_params=pltpu.CompilerParams(vmem_limit_bytes=limit),
        name="project",
    )(*operands, *others)


def score_kernel(inp_size, pair, queries, ring, *refs):
    near_ref, refs = refs[0], refs[1:]
    if inp_size > pair:
        far_ref, refs = refs[0], refs[1:]
    *a_refs, out_ref, held, sems = refs
    blocks, shard, width = held.shape[1:]
    me, here = lax.axis_index("inp"), lax.axis_index("out")
    sources = []
    for number in range(inp_size):
        by, other = divmod(number, pair)
        source = lax.rem(me - pair * by + inp_size, inp_size)
        sources.append(jnp.bitwise_xor(source, other) if pair == 2 else source)

    def bring(number):
        source = sources[number]
        if len(a_refs) == 1:
            begin = pl.multiple_of(source * shard, shard)
            pltpu.make_async_copy(
                a_refs[0].at[:, pl.ds(begin, shard), :], held.at[number], sems.at[number]
            ).start()
            return
        for at, a_ref in enumerate(a_refs):
            for place, spot in enumerate(ring):

                @pl.when((here == spot) & (source == ring[place - at]))
                def _(a_ref=a_ref):
                    pltpu.make_async_copy(a_ref, held.at[number], sems.at[number]).start()

    lanes = 128
    bring(0)
    for number, source in enumerate(sources):
        if number + 1 < inp_size:
            bring(number + 1)
        pltpu.make_async_copy(held.at[number], held.at[number], sems.at[number]).wait()
        totals = [None] * queries
        begin = (number if number < pair else number - pair) * blocks * shard
        for at in range(0, width, lanes):
            block = held[number, :, :, at:at + lanes].reshape(blocks * shard, lanes).astype(jnp.float32)
            for query in range(queries):
                where = (slice(begin, begin + blocks * shard), slice(at, at + lanes))
                rows = (near_ref if number < pair else far_ref)[(query, *where)]
                term = rows * block
                totals[query] = term if totals[query] is None else totals[query] + term
        for query in range(queries):
            out_ref[source, query, :] = jnp.sum(totals[query].T, axis=0)


def score(sums, slots, ring, inp_size, pair, queries, blocks, shard):
    width = sums[0].shape[2]
    return pl.pallas_call(
        functools.partial(score_kernel, inp_size, pair, queries, ring),
        in_specs=[pl.BlockSpec(memory_space=pltpu.VMEM)] * len(sums)
        + [pl.BlockSpec(memory_space=pl.ANY)] * len(slots),
        out_specs=pl.BlockSpec(memory_space=pltpu.VMEM),
        out_shape=jax.ShapeDtypeStruct((inp_size, queries, blocks * shard), jnp.float32),
        scratch_shapes=[
            pltpu.VMEM((inp_size, blocks, shard, width), jnp.bfloat16),
            pltpu.SemaphoreType.DMA((inp_size,)),
        ],
        compiler_params=pltpu.CompilerParams(vmem_limit_bytes=6 * 1024 * 1024),
        name="score",
    )(*sums, *slots)


def xor_sum(value, axis, size):
    if size & (size - 1):
        return lax.psum(value, axis)
    terms = [value]
    for other in range(1, size):
        terms.append(lax.ppermute(value, axis, [(at, at ^ other) for at in range(size)]))
    while len(terms) > 1:
        terms = [terms[at] + terms[at + 1] for at in range(0, len(terms), 2)]
    return terms[0]


def after(value, *others):
    any_spec = pl.BlockSpec(memory_space=pl.ANY)
    return pl.pallas_call(
        lambda *refs: None,
        in_specs=[any_spec] * (1 + len(others)),
        out_specs=any_spec,
        out_shape=jax.ShapeDtypeStruct(value.shape, value.dtype),
        input_output_aliases={0: 0},
        compiler_params=pltpu.CompilerParams(vmem_limit_bytes=HELPER_VMEM),
        name="after",
    )(pltpu.with_memory_space_constraint(value, pltpu.VMEM), *others)


def halve_kernel(source_ref, *refs):
    *outs, sems = refs[-3:]
    begin, copies = 0, []
    for at, out_ref in enumerate(outs):
        where = source_ref.at[:, pl.ds(begin, out_ref.shape[1])]
        copies.append(pltpu.make_async_copy(where, out_ref, sems.at[at]))
        begin += out_ref.shape[1]
    run(copies, True)
    run(copies, False)


def halve(value, *others):
    rows, columns = value.shape
    first = columns // 256 * 128 or columns
    if first == columns:
        return [after(value, *others)]
    return pl.pallas_call(
        halve_kernel,
        in_specs=[pl.BlockSpec(memory_space=pl.ANY)] * (1 + len(others)),
        out_specs=[pl.BlockSpec(memory_space=pltpu.VMEM)] * 2,
        out_shape=[jax.ShapeDtypeStruct((rows, part), value.dtype) for part in (first, columns - first)],
        scratch_shapes=[pltpu.SemaphoreType.DMA((2,))],
        cost_estimate=pl.CostEstimate(flops=1024, bytes_accessed=1024, transcendentals=0),
        compiler_params=pltpu.CompilerParams(vmem_limit_bytes=HELPER_VMEM),
        name="halve",
    )(pltpu.with_memory_space_constraint(value, pltpu.VMEM), *others)


def in_hbm(value):
    return pltpu.with_memory_space_constraint(value, pltpu.HBM)


def cut_kernel(spans, total, source_ref, a_ref, *refs):
    outs, sems = refs[-1 - total:-1], refs[-1]
    copies = []
    for at, out_ref in enumerate(outs):
        piece = source_ref.at[:, pl.ds(*spans[at])] if at < len(spans) else a_ref
        copies.append(pltpu.make_async_copy(piece, out_ref, sems.at[at]))
    run(copies, True)
    run(copies, False)


def cut(source, spans, activations, copied, *others):
    shapes = [(source.shape[0], length) for _, length in spans] + [activations.shape] * copied
    return pl.pallas_call(
        functools.partial(cut_kernel, spans, len(shapes)),
        in_specs=[pl.BlockSpec(memory_space=pl.ANY)] * (2 + len(others)),
        out_specs=[pl.BlockSpec(memory_space=pltpu.VMEM)] * len(shapes),
        out_shape=[jax.ShapeDtypeStruct(shape, source.dtype) for shape in shapes],
        scratch_shapes=[pltpu.SemaphoreType.DMA((len(shapes),))],
        compiler_params=pltpu.CompilerParams(vmem_limit_bytes=HELPER_VMEM),
        name="cut",
    )(source, activations, *others)


def shards(inp_size, out_size, activations, out_grads, query_grads, token_ids, loss_mask):
    blocks, shard, depth = out_grads.shape
    queries, _, width = query_grads.shape
    tokens = token_ids.shape[1]
    pair = 2 if inp_size % 2 == 0 else 1
    chips = inp_size // pair
    rows = blocks * shard

    unit = 256 if depth % 256 == 0 else depth
    units = depth // unit
    edges = [0]
    for at in range(len(WEIGHTS)):
        edges.append(units * sum(WEIGHTS[:at + 1]) // sum(WEIGHTS) * unit)
    spans = [(begin, end - begin) for begin, end in zip(edges, edges[1:]) if end > begin]
    chunks = len(spans)

    def flip(value):
        return lax.ppermute(value, "inp", [(at, at ^ 1) for at in range(inp_size)])

    def shift(value, by):
        return lax.ppermute(value, "inp", [(at, (at + pair * by) % inp_size) for at in range(inp_size)])

    own = in_hbm(out_grads.reshape(rows, depth))
    near = [pltpu.with_memory_space_constraint(flip(own), pltpu.VMEM)] if pair == 2 else []
    query_grads = in_hbm(query_grads)
    activations = in_hbm(activations)
    line = inp_size == out_size and activations.shape[1] == shard and out_size > 1
    ring = list(range(0, out_size, 2)) + list(range(1, out_size, 2))[::-1]
    turn = [(ring[at - 1], ring[at]) for at in range(out_size)]
    pieces_out = list(cut(own, spans[:1], activations, False)) if chips > 1 else []
    *rest, moving = cut(own, spans[1:] if chips > 1 else [], activations, True, *pieces_out)
    pieces_out += rest

    slots = [moving]
    if line:
        slots.append(lax.ppermute(moving, "out", turn))
    else:
        slots = [lax.all_gather(activations, "out", axis=1, tiled=True)]

    def step_along(mark):
        if not line or len(slots) == out_size:
            return []
        slots[-1] = ended = after(slots[-1], mark)
        slots.append(lax.ppermute(ended, "out", turn))
        return [ended]

    coming = []
    if chips > 1:
        coming = [[shift(piece, by) for by in range(1, chips)] for piece in pieces_out]
    waiting = []

    def receive(mark, count=1):
        ended = []
        for _ in range(min(count, len(coming))):
            pieces = [halve(piece, mark, *sum(waiting, [])) for piece in coming.pop(0)]
            parts = []
            for halves in zip(*pieces):
                for half in halves:
                    parts += [half, flip(half)] if pair == 2 else [half]
            waiting.append(parts)
            ended += [halves[0] for halves in pieces]
        return ended

    room = depth
    near_plan = plan_of(queries, 0, depth, width, depth)
    early = near_plan.steps * 3 // 8 * 2 or near_plan.steps
    plans = [near_plan._replace(steps=early)]
    if early < near_plan.steps:
        plans.append(near_plan._replace(first=early, steps=near_plan.steps - early))
    far_plans = [plan_of(queries, begin, length, width, room) for begin, length in spans] if chips > 1 else []

    calls = [("near", plans[0], 0), *[("far", plan, 1) for plan in far_plans[:1]]]
    calls += [("near", plan, min(1, len(far_plans[1:]))) for plan in plans[1:]]
    calls += [("far", plan, 0 if at == 0 and len(plans) > 1 else 1) for at, plan in enumerate(far_plans[1:])]

    slot, laid = load(pieces_out or [own], pair * rows, query_grads, plans[0], room)
    near_sum = far_sum = None
    for at, (kind, plan, count) in enumerate(calls):
        later = calls[at + 1][1] if at + 1 < len(calls) else None
        others = receive(mark, count) if at > 0 else []
        if kind == "far" and count:
            others += step_along(mark)
        if kind == "far" and any(later_kind == "near" for later_kind, _, _ in calls[at:]):
            others.append(pltpu.with_memory_space_constraint(laid, pltpu.VMEM))
        if kind == "near":
            near_sum, mark, slot, laid = project(
                near if at == 0 else [], pair * rows, query_grads, plan, later, slot, near_sum, others, laid
            )
        else:
            far_sum, mark, slot = project(
                waiting.pop(0), (inp_size - pair) * rows, query_grads, plan, later, slot, far_sum, others
            )
    sums = [near_sum] + ([] if far_sum is None else [far_sum])
    raw = score(sums, slots, ring, inp_size, pair, queries, blocks, shard)
    raw = raw.reshape(inp_size, queries, blocks, shard).transpose(1, 2, 0, 3).reshape(queries, blocks, tokens)
    raw = xor_sum(xor_sum(raw, "inp", inp_size), "out", out_size)
    equal = token_ids[:, :, None] == token_ids[:, None, :]
    counts = jnp.sum(equal.astype(jnp.int32), axis=2)
    weight = loss_mask.astype(jnp.float32) / counts.astype(jnp.float32)
    return raw * weight[None]


def solution(mesh):
    in_specs = (
        P("grp", "out", "inp"),
        P("grp", "inp", "out"),
        P(None, "out", "inp"),
        P("grp", None),
        P("grp", None),
    )
    out_specs = P(None, "grp", None)
    body = functools.partial(shards, mesh.shape["inp"], mesh.shape["out"])
    return jax.shard_map(body, mesh=mesh, in_specs=in_specs, out_specs=out_specs, check_vma=False)
```

```python
import functools
import typing

import jax
import jax.numpy as jnp
from jax import lax
from jax.experimental import pallas as pl
from jax.experimental.pallas import tpu as pltpu
from jax.sharding import PartitionSpec as P

WEIGHTS = (10, 7, 5, 6)
HELPER_VMEM = 1024 * 1024
TILE = 512


def tile_of(length, most):
    size = min(length, most)
    while length % size:
        size -= 128
    return size


class Plan(typing.NamedTuple):
    first: int
    steps: int
    begin: int
    depth: int
    tile: int
    strips: int
    turns: int


def plan_of(queries, begin, depth, width, room):
    tile = tile_of(width, TILE)
    strips = 1
    while strips * 2 * depth <= room and width // tile % (strips * 2) == 0:
        strips *= 2
    turns = width // tile // strips
    return Plan(0, queries * turns, begin, depth, tile, strips, turns)


def fetches(plan, step, q_ref, slot_ref, sems):
    number, turn = (plan.first + step) // plan.turns, (plan.first + step) % plan.turns
    copies = []
    for strip in range(plan.strips):
        column = (turn * plan.strips + strip) * plan.tile
        if not isinstance(column, int):
            column = pl.multiple_of(column, plan.tile)
        source = q_ref.at[number, pl.ds(plan.begin, plan.depth), pl.ds(column, plan.tile)]
        target = slot_ref.at[pl.ds(strip * plan.depth, plan.depth)]
        copies.append(pltpu.make_async_copy(source, target, sems.at[strip]))
    return copies


def run(copies, start):
    for copy in copies:
        if start:
            copy.start()
        else:
            copy.wait()


def load_kernel(plan, parts, *refs):
    g_refs, (q_ref, slot_ref, x_ref, sems, slot_sems) = refs[:parts], refs[parts:]
    copies = fetches(plan, 0, q_ref, slot_ref, slot_sems)
    column = 0
    for at, g_ref in enumerate(g_refs):
        rows, columns = g_ref.shape
        where = x_ref.at[pl.ds(0, rows), pl.ds(column, columns)]
        copies.append(pltpu.make_async_copy(g_ref, where, sems.at[at]))
        column += columns
    run(copies, True)
    run(copies, False)


def load(own, total, query_grads, plan, room):
    vmem_spec = pl.BlockSpec(memory_space=pltpu.VMEM)
    depth = sum(part.shape[1] for part in own)
    return pl.pallas_call(
        functools.partial(load_kernel, plan, len(own)),
        in_specs=[pl.BlockSpec(memory_space=pl.ANY)] * (len(own) + 1),
        out_specs=[vmem_spec] * 2,
        out_shape=[
            jax.ShapeDtypeStruct((room, plan.tile), jnp.bfloat16),
            jax.ShapeDtypeStruct((total, depth), jnp.bfloat16),
        ],
        scratch_shapes=[pltpu.SemaphoreType.DMA((len(own),)), pltpu.SemaphoreType.DMA((plan.strips,))],
        cost_estimate=pl.CostEstimate(flops=1024, bytes_accessed=1024, transcendentals=0),
        compiler_params=pltpu.CompilerParams(vmem_limit_bytes=HELPER_VMEM),
        name="load",
    )(*own, query_grads)


def project_kernel(parts, plan, later, add, laid, *refs):
    g_refs, q_ref = refs[:parts], refs[parts]
    sum_ref, mark_ref, slot_a, x_ref, slot_b, sems, sems_a, sems_b = refs[-8:]
    total = x_ref.shape[0]
    copies = []
    together = total // g_refs[0].shape[0] if parts and not laid else 1
    column = 0
    for at, g_ref in enumerate(g_refs):
        rows = g_ref.shape[0]
        row = total - rows if laid else at % together * rows
        where = x_ref.at[pl.ds(row, rows), pl.ds(column, g_ref.shape[1])]
        copies.append(pltpu.make_async_copy(g_ref, where, sems.at[at]))
        if not laid and at % together == together - 1:
            column += g_ref.shape[1]
    steps = plan.steps
    run(copies, True)
    if steps > 1:
        run(fetches(plan, 1, q_ref, slot_b, sems_b), True)
    mark_ref[...] = jnp.zeros_like(mark_ref)
    run(copies, False)

    def multiply(step, slot_ref):
        number, turn = (plan.first + step) // plan.turns, (plan.first + step) % plan.turns
        for strip in range(plan.strips):
            product = jnp.dot(
                x_ref[...],
                slot_ref[strip * plan.depth:(strip + 1) * plan.depth, :],
                preferred_element_type=jnp.float32,
            )
            begin = (turn * plan.strips + strip) * plan.tile
            if not isinstance(begin, int):
                begin = pl.multiple_of(begin, plan.tile)
            where = (number, slice(None), pl.ds(begin, plan.tile))
            if add:
                sum_ref[where] += product
            else:
                sum_ref[where] = product

    def both(pair):
        step = pair * 2

        @pl.when(pair > 0)
        def _():
            run(fetches(plan, step + 1, q_ref, slot_b, sems_b), True)
            run(fetches(plan, step, q_ref, slot_a, sems_a), False)

        multiply(step, slot_a)

        @pl.when(step + 2 < steps)
        def _():
            run(fetches(plan, step + 2, q_ref, slot_a, sems_a), True)

        if later is not None:

            @pl.when(step + 2 >= steps)
            def _():
                run(fetches(later, 0, q_ref, slot_a, sems_a), True)

        run(fetches(plan, step + 1, q_ref, slot_b, sems_b), False)
        multiply(step + 1, slot_b)

    if steps % 2 == 0:

        @pl.loop(0, steps // 2)
        def _(pair):
            both(pair)
    else:
        for step in range(steps):
            slot_ref, slot_sems = (slot_a, sems_a) if step % 2 == 0 else (slot_b, sems_b)
            if step > 0:
                run(fetches(plan, step, q_ref, slot_ref, slot_sems), step > 1)
                if step > 1:
                    run(fetches(plan, step, q_ref, slot_ref, slot_sems), False)
            multiply(step, slot_ref)
        if later is not None:
            run(fetches(later, 0, q_ref, slot_a, sems_a), True)
    if later is not None:
        run(fetches(later, 0, q_ref, slot_a, sems_a), False)


def project(parts, rows, query_grads, plan, later, slot, running, others=(), laid=None):
    queries, _, width = query_grads.shape
    fresh = running is None
    any_spec = pl.BlockSpec(memory_space=pl.ANY)
    vmem_spec = pl.BlockSpec(memory_space=pltpu.VMEM)
    operands = [*parts, query_grads, slot]
    in_specs = [any_spec] * (len(parts) + 1) + [vmem_spec]
    aliases = {len(parts) + 1: 2}
    if not fresh:
        aliases[len(operands)] = 0
        operands.append(running)
        in_specs.append(vmem_spec)
    out_shape = [
        jax.ShapeDtypeStruct((queries, rows, width), jnp.float32),
        jax.ShapeDtypeStruct((8, 128), jnp.float32),
        jax.ShapeDtypeStruct(slot.shape, slot.dtype),
    ]
    scratch = []
    if laid is not None:
        aliases[len(operands)] = 3
        operands.append(laid)
        in_specs.append(vmem_spec)
        out_shape.append(jax.ShapeDtypeStruct(laid.shape, laid.dtype))
    else:
        scratch.append(pltpu.VMEM((rows, plan.depth), jnp.bfloat16))
    scratch += [
        pltpu.VMEM(slot.shape, slot.dtype),
        pltpu.SemaphoreType.DMA((max(len(parts), 1),)),
        pltpu.SemaphoreType.DMA((max(plan.strips, later.strips if later else 1),)),
        pltpu.SemaphoreType.DMA((plan.strips,)),
    ]
    limit = 2 * slot.size + (2 * rows * plan.depth if laid is None else 0) + 3 * 1024 * 1024
    return pl.pallas_call(
        functools.partial(
            project_kernel, len(parts), plan, later, not fresh and laid is None, laid is not None
        ),
        in_specs=in_specs + [any_spec] * len(others),
        out_specs=[vmem_spec] * len(out_shape),
        out_shape=out_shape,
        scratch_shapes=scratch,
        input_output_aliases=aliases,
        cost_estimate=pl.CostEstimate(flops=1024, bytes_accessed=1024, transcendentals=0),
        compiler_params=pltpu.CompilerParams(vmem_limit_bytes=limit),
        name="project",
    )(*operands, *others)


def score_kernel(inp_size, pair, queries, ring, *refs):
    near_ref, refs = refs[0], refs[1:]
    if inp_size > pair:
        far_ref, refs = refs[0], refs[1:]
    *a_refs, out_ref, held, sems = refs
    blocks, shard, width = held.shape[1:]
    me, here = lax.axis_index("inp"), lax.axis_index("out")
    sources = []
    for number in range(inp_size):
        by, other = divmod(number, pair)
        source = lax.rem(me - pair * by + inp_size, inp_size)
        sources.append(jnp.bitwise_xor(source, other) if pair == 2 else source)

    def bring(number):
        source = sources[number]
        if len(a_refs) == 1:
            begin = pl.multiple_of(source * shard, shard)
            pltpu.make_async_copy(
                a_refs[0].at[:, pl.ds(begin, shard), :], held.at[number], sems.at[number]
            ).start()
            return
        for at, a_ref in enumerate(a_refs):
            for place, spot in enumerate(ring):

                @pl.when((here == spot) & (source == ring[place - at]))
                def _(a_ref=a_ref):
                    pltpu.make_async_copy(a_ref, held.at[number], sems.at[number]).start()

    lanes = 128
    bring(0)
    for number, source in enumerate(sources):
        if number + 1 < inp_size:
            bring(number + 1)
        pltpu.make_async_copy(held.at[number], held.at[number], sems.at[number]).wait()
        totals = [None] * queries
        begin = (number if number < pair else number - pair) * blocks * shard
        for at in range(0, width, lanes):
            block = held[number, :, :, at:at + lanes].reshape(blocks * shard, lanes).astype(jnp.float32)
            for query in range(queries):
                where = (slice(begin, begin + blocks * shard), slice(at, at + lanes))
                rows = (near_ref if number < pair else far_ref)[(query, *where)]
                term = rows * block
                totals[query] = term if totals[query] is None else totals[query] + term
        for query in range(queries):
            out_ref[source, query, :] = jnp.sum(totals[query].T, axis=0)


def score(sums, slots, ring, inp_size, pair, queries, blocks, shard):
    width = sums[0].shape[2]
    return pl.pallas_call(
        functools.partial(score_kernel, inp_size, pair, queries, ring),
        in_specs=[pl.BlockSpec(memory_space=pltpu.VMEM)] * len(sums)
        + [pl.BlockSpec(memory_space=pl.ANY)] * len(slots),
        out_specs=pl.BlockSpec(memory_space=pltpu.VMEM),
        out_shape=jax.ShapeDtypeStruct((inp_size, queries, blocks * shard), jnp.float32),
        scratch_shapes=[
            pltpu.VMEM((inp_size, blocks, shard, width), jnp.bfloat16),
            pltpu.SemaphoreType.DMA((inp_size,)),
        ],
        compiler_params=pltpu.CompilerParams(vmem_limit_bytes=6 * 1024 * 1024),
        name="score",
    )(*sums, *slots)


def xor_sum(value, axis, size):
    if size & (size - 1):
        return lax.psum(value, axis)
    terms = [value]
    for other in range(1, size):
        terms.append(lax.ppermute(value, axis, [(at, at ^ other) for at in range(size)]))
    while len(terms) > 1:
        terms = [terms[at] + terms[at + 1] for at in range(0, len(terms), 2)]
    return terms[0]


def after(value, *others):
    any_spec = pl.BlockSpec(memory_space=pl.ANY)
    return pl.pallas_call(
        lambda *refs: None,
        in_specs=[any_spec] * (1 + len(others)),
        out_specs=any_spec,
        out_shape=jax.ShapeDtypeStruct(value.shape, value.dtype),
        input_output_aliases={0: 0},
        compiler_params=pltpu.CompilerParams(vmem_limit_bytes=HELPER_VMEM),
        name="after",
    )(pltpu.with_memory_space_constraint(value, pltpu.VMEM), *others)


def halve_kernel(source_ref, *refs):
    *outs, sems = refs[-3:]
    begin, copies = 0, []
    for at, out_ref in enumerate(outs):
        where = source_ref.at[:, pl.ds(begin, out_ref.shape[1])]
        copies.append(pltpu.make_async_copy(where, out_ref, sems.at[at]))
        begin += out_ref.shape[1]
    run(copies, True)
    run(copies, False)


def halve(value, *others):
    rows, columns = value.shape
    first = columns // 256 * 128 or columns
    if first == columns:
        return [after(value, *others)]
    return pl.pallas_call(
        halve_kernel,
        in_specs=[pl.BlockSpec(memory_space=pl.ANY)] * (1 + len(others)),
        out_specs=[pl.BlockSpec(memory_space=pltpu.VMEM)] * 2,
        out_shape=[jax.ShapeDtypeStruct((rows, part), value.dtype) for part in (first, columns - first)],
        scratch_shapes=[pltpu.SemaphoreType.DMA((2,))],
        cost_estimate=pl.CostEstimate(flops=1024, bytes_accessed=1024, transcendentals=0),
        compiler_params=pltpu.CompilerParams(vmem_limit_bytes=HELPER_VMEM),
        name="halve",
    )(pltpu.with_memory_space_constraint(value, pltpu.VMEM), *others)


def in_hbm(value):
    return pltpu.with_memory_space_constraint(value, pltpu.HBM)


def cut_kernel(spans, total, source_ref, a_ref, *refs):
    outs, sems = refs[-1 - total:-1], refs[-1]
    copies = []
    for at, out_ref in enumerate(outs):
        piece = source_ref.at[:, pl.ds(*spans[at])] if at < len(spans) else a_ref
        copies.append(pltpu.make_async_copy(piece, out_ref, sems.at[at]))
    run(copies, True)
    run(copies, False)


def cut(source, spans, activations, copied, *others):
    shapes = [(source.shape[0], length) for _, length in spans] + [activations.shape] * copied
    return pl.pallas_call(
        functools.partial(cut_kernel, spans, len(shapes)),
        in_specs=[pl.BlockSpec(memory_space=pl.ANY)] * (2 + len(others)),
        out_specs=[pl.BlockSpec(memory_space=pltpu.VMEM)] * len(shapes),
        out_shape=[jax.ShapeDtypeStruct(shape, source.dtype) for shape in shapes],
        scratch_shapes=[pltpu.SemaphoreType.DMA((len(shapes),))],
        compiler_params=pltpu.CompilerParams(vmem_limit_bytes=HELPER_VMEM),
        name="cut",
    )(source, activations, *others)


def shards(inp_size, out_size, activations, out_grads, query_grads, token_ids, loss_mask):
    blocks, shard, depth = out_grads.shape
    queries, _, width = query_grads.shape
    tokens = token_ids.shape[1]
    pair = 2 if inp_size % 2 == 0 else 1
    chips = inp_size // pair
    rows = blocks * shard

    unit = 256 if depth % 256 == 0 else depth
    units = depth // unit
    edges = [0]
    for at in range(len(WEIGHTS)):
        edges.append(units * sum(WEIGHTS[:at + 1]) // sum(WEIGHTS) * unit)
    spans = [(begin, end - begin) for begin, end in zip(edges, edges[1:]) if end > begin]
    chunks = len(spans)

    def flip(value):
        return lax.ppermute(value, "inp", [(at, at ^ 1) for at in range(inp_size)])

    def shift(value, by):
        return lax.ppermute(value, "inp", [(at, (at + pair * by) % inp_size) for at in range(inp_size)])

    own = in_hbm(out_grads.reshape(rows, depth))
    near = [pltpu.with_memory_space_constraint(flip(own), pltpu.VMEM)] if pair == 2 else []
    query_grads = in_hbm(query_grads)
    activations = in_hbm(activations)
    line = inp_size == out_size and activations.shape[1] == shard and out_size > 1
    ring = list(range(0, out_size, 2)) + list(range(1, out_size, 2))[::-1]
    turn = [(ring[at - 1], ring[at]) for at in range(out_size)]
    pieces_out = list(cut(own, spans[:1], activations, False)) if chips > 1 else []
    *rest, moving = cut(own, spans[1:] if chips > 1 else [], activations, True, *pieces_out)
    pieces_out += rest

    slots = [moving]
    if line:
        slots.append(lax.ppermute(moving, "out", turn))
    else:
        slots = [lax.all_gather(activations, "out", axis=1, tiled=True)]

    def step_along(mark):
        if not line or len(slots) == out_size:
            return []
        slots[-1] = ended = after(slots[-1], mark)
        slots.append(lax.ppermute(ended, "out", turn))
        return [ended]

    coming = []
    if chips > 1:
        coming = [[shift(piece, by) for by in range(1, chips)] for piece in pieces_out]
    waiting = []

    def receive(mark, count=1):
        ended = []
        for _ in range(min(count, len(coming))):
            pieces = [halve(piece, mark, *sum(waiting, [])) for piece in coming.pop(0)]
            parts = []
            for halves in zip(*pieces):
                for half in halves:
                    parts += [half, flip(half)] if pair == 2 else [half]
            waiting.append(parts)
            ended += [halves[0] for halves in pieces]
        return ended

    room = depth
    near_plan = plan_of(queries, 0, depth, width, depth)
    early = near_plan.steps * 3 // 8 * 2 or near_plan.steps
    plans = [near_plan._replace(steps=early)]
    if early < near_plan.steps:
        plans.append(near_plan._replace(first=early, steps=near_plan.steps - early))
    far_plans = [plan_of(queries, begin, length, width, room) for begin, length in spans] if chips > 1 else []

    calls = [("near", plans[0], 0), *[("far", plan, 1) for plan in far_plans[:1]]]
    calls += [("near", plan, min(1, len(far_plans[1:]))) for plan in plans[1:]]
    calls += [("far", plan, 0 if at == 0 and len(plans) > 1 else 1) for at, plan in enumerate(far_plans[1:])]

    slot, laid = load(pieces_out or [own], pair * rows, query_grads, plans[0], room)
    near_sum = far_sum = None
    for at, (kind, plan, count) in enumerate(calls):
        later = calls[at + 1][1] if at + 1 < len(calls) else None
        others = receive(mark, count) if at > 0 else []
        if kind == "far":
            others += step_along(mark)
        if kind == "far" and any(later_kind == "near" for later_kind, _, _ in calls[at:]):
            others.append(pltpu.with_memory_space_constraint(laid, pltpu.VMEM))
        if kind == "near":
            near_sum, mark, slot, laid = project(
                near if at == 0 else [], pair * rows, query_grads, plan, later, slot, near_sum, others, laid
            )
        else:
            far_sum, mark, slot = project(
                waiting.pop(0), (inp_size - pair) * rows, query_grads, plan, later, slot, far_sum, others
            )
    sums = [near_sum] + ([] if far_sum is None else [far_sum])
    raw = score(sums, slots, ring, inp_size, pair, queries, blocks, shard)
    raw = raw.reshape(inp_size, queries, blocks, shard).transpose(1, 2, 0, 3).reshape(queries, blocks, tokens)
    raw = xor_sum(xor_sum(raw, "inp", inp_size), "out", out_size)
    equal = token_ids[:, :, None] == token_ids[:, None, :]
    counts = jnp.sum(equal.astype(jnp.int32), axis=2)
    weight = loss_mask.astype(jnp.float32) / counts.astype(jnp.float32)
    return raw * weight[None]


def solution(mesh):
    in_specs = (
        P("grp", "out", "inp"),
        P("grp", "inp", "out"),
        P(None, "out", "inp"),
        P("grp", None),
        P("grp", None),
    )
    out_specs = P(None, "grp", None)
    body = functools.partial(shards, mesh.shape["inp"], mesh.shape["out"])
    return jax.shard_map(body, mesh=mesh, in_specs=in_specs, out_specs=out_specs, check_vma=False)
```
